128 devices in a mesh: owner: 32 (over x, z, core), seq: 4 (over y).
Axes of the slice: x: 4, y: 4, z: 4, core: 2. Of those that a mesh axis runs over, the one named last changes fastest.
Arguments:
- cand_features: bfloat16 [16384, 1024], P(('owner', 'seq')), may hold values from -6 to 6
- owner_route: int32 [16384], P(('owner', 'seq')), may hold values from 0 to 31, as said below
- hist_lengths: int32 [32], P('owner'), may hold values from 4096 to 16384, as said below
- hist_keys: bfloat16 [32, 16384, 1024], P('owner', 'seq'), may hold values from -6 to 6
- hist_values: bfloat16 [32, 16384, 1024], P('owner', 'seq'), may hold values from -40 to 40
- query_weight: bfloat16 [1024, 1024], replicated, may hold values from -0.1875 to 0.1875
- gate_weight: bfloat16 [1024, 1024], replicated, may hold values from -0.1875 to 0.1875
- out_weight: bfloat16 [1024, 1024], replicated, may hold values from -0.1875 to 0.1875
Outputs:
- ranked: bfloat16 [16384, 1024], P(('owner', 'seq'))
The draws below stay inside these ranges and needn't reach their ends.
Inputs may be any that keep to these rules, and one draw needn't show every extreme that they name: `owner_route`: among the rows of one device, at most 8 name one owner group; one owner group is named by exactly 8 rows of every device. `hist_lengths`: multiples of 128; some user has 16384.
All inputs are finite; a program needn't handle non-finite values.
Results may differ from the reference program's by a relative error of at most 0.013.
Values may be sent and summed in bfloat16 or wider, within the bound.
A program may use at most 128 MiB of HBM per device.

```python
import math
import jax
import jax.numpy as jnp
from jax import lax

D = 1024
HEADS = 8
HIST = 16384
TOK_DEV = 128
CAP = 8
USERS = 32
EV_DEV = 4096
CANDS = 16384
N_OWNER = 32
N_SEQ = 4


def draw_owner_route(key, part):
    key = jax.random.fold_in(key, 7)
    hot_key, favour_key, noise_key, order_key = jax.random.split(key, 4)
    slot_count = N_OWNER * CAP
    block_count = N_OWNER * N_SEQ
    slot_owner = jnp.arange(slot_count, dtype=jnp.int32) // CAP
    slot_ids = jnp.arange(slot_count, dtype=jnp.int32)
    hottest = jax.random.randint(hot_key, (), 0, N_OWNER)
    favour = jax.random.randint(favour_key, (N_OWNER,), 0, 4)
    noise = jax.random.randint(noise_key, (block_count, slot_count), 0, 1024)
    scores = (favour[slot_owner][None, :] * 1024 + noise) * 4096 + slot_ids[None, :]
    assured = jnp.arange(block_count, dtype=jnp.int32) % N_OWNER * CAP
    scores = jnp.where(slot_ids[None, :] == assured[:, None], (1 << 29) + slot_ids[None, :], scores)
    scores = jnp.where(slot_owner[None, :] == hottest, (1 << 30) + slot_ids[None, :], scores)
    top_scores, chosen = lax.top_k(scores, TOK_DEV)
    owners = slot_owner[chosen]
    mixing = jax.random.randint(order_key, (block_count, TOK_DEV), 0, 4096) * 4096 + jnp.arange(TOK_DEV, dtype=jnp.int32)[None, :]
    shuffle = jnp.argsort(mixing, axis=1, stable=True)
    return jnp.take_along_axis(owners, shuffle, axis=1).reshape(block_count * TOK_DEV).astype(jnp.int32)


def draw_hist_lengths(key, part):
    key = jax.random.fold_in(key, 9)
    count_key, place_key = jax.random.split(key)
    blocks_each = jax.random.randint(count_key, (USERS,), HIST // 512, HIST // 128 + 1)
    fullest = jax.random.randint(place_key, (), 0, USERS)
    blocks_each = jnp.where(jnp.arange(USERS, dtype=jnp.int32) == fullest, HIST // 128, blocks_each)
    return (blocks_each * 128).astype(jnp.int32)


def draw_hist_values(key, part):
    key = jax.random.fold_in(key, 11)
    base_key, column_key, event_key = jax.random.split(key, 3)
    base = jax.random.truncated_normal(base_key, -4.0, 4.0, (USERS, HIST, D), jnp.float32)
    spread = math.log(10.0)
    columns = jnp.exp(jax.random.uniform(column_key, (D,), jnp.float32, 0.0, spread))
    events = jnp.exp(jax.random.uniform(event_key, (USERS, HIST, 1), jnp.float32, 0.0, math.log(10.0)))
    return (base * columns * events / 16.0).astype(jnp.bfloat16)


def level_of(key, dims, pieces, least, high):
    level = 1.0
    for axis_at, shards_of in pieces:
        heights = jax.random.uniform(jax.random.fold_in(jax.random.fold_in(key, 6), axis_at), (shards_of,), jnp.float32, least / len(pieces), high / len(pieces))
        level = level * jnp.repeat(jnp.exp(heights), dims[axis_at] // shards_of).reshape((-1,) + (1,) * (len(dims) - 1 - axis_at))
    return level


def scatter_about(key, shape, width, most, pieces=(), held_as=jnp.bfloat16):
    values = width * jax.random.normal(key, shape, jnp.float32)
    if pieces:
        values = values * level_of(key, shape, pieces, -0.22, 0.18)
    return jnp.clip(values, -most, most).astype(held_as)


def setup_inputs(seed: int = 0) -> dict:
    keys = jax.random.split(jax.random.key(seed), 9)
    return {
        "cand_features": scatter_about(keys[0], (CANDS, D), 1.0, 6.0, ((0, 128),)),
        "owner_route": draw_owner_route(jax.random.fold_in(keys[8], 71), 0),
        "hist_lengths": draw_hist_lengths(jax.random.fold_in(keys[8], 71), 0),
        "hist_keys": scatter_about(keys[3], (USERS, HIST, D), 1.0, 6.0, ((0, 32), (1, 4))),
        "hist_values": draw_hist_values(jax.random.fold_in(keys[8], 71), 0),
        "query_weight": scatter_about(keys[5], (D, D), D ** -0.5, 0.1875),
        "gate_weight": scatter_about(keys[6], (D, D), D ** -0.5, 0.1875),
        "out_weight": scatter_about(keys[7], (D, D), D ** -0.5, 0.1875),
    }


def reference(cand_features, owner_route, hist_lengths, hist_keys, hist_values, query_weight, gate_weight, out_weight):
    feature_width = cand_features.shape[1]
    head_width = feature_width // HEADS
    most_rows = 2 * TOK_DEV * N_SEQ
    scaling = head_width ** (-0.5)

    def per_user(user):
        picked = jnp.nonzero(owner_route == user, size=most_rows, fill_value=CANDS)[0].astype(jnp.int32)
        chosen = jnp.take(cand_features, jnp.minimum(picked, CANDS - 1), axis=0)
        query = jnp.dot(chosen, query_weight, preferred_element_type=jnp.float32).astype(jnp.bfloat16)
        query = lax.optimization_barrier(query).astype(jnp.float32).reshape(most_rows, HEADS, head_width)
        gate = jax.nn.silu(jnp.dot(chosen, gate_weight, preferred_element_type=jnp.float32))
        length = hist_lengths[user]
        user_keys = hist_keys[user]
        user_values = hist_values[user]
        attended = jnp.zeros((most_rows, feature_width), jnp.float32)
        for block_id in range(N_SEQ):
            key_part = user_keys[block_id * EV_DEV:(block_id + 1) * EV_DEV].astype(jnp.float32).reshape(EV_DEV, HEADS, head_width)
            value_part = user_values[block_id * EV_DEV:(block_id + 1) * EV_DEV].astype(jnp.float32).reshape(EV_DEV, HEADS, head_width)
            score = jnp.einsum('chd,ehd->hce', query, key_part) * scaling
            position = block_id * EV_DEV + jnp.arange(EV_DEV, dtype=jnp.int32)
            weight = jnp.where(position[None, None, :] < length, jax.nn.silu(score), 0.0).astype(jnp.bfloat16)
            weight = lax.optimization_barrier(weight).astype(jnp.float32)
            partial_value = jnp.einsum('hce,ehd->chd', weight, value_part).reshape(most_rows, feature_width).astype(jnp.bfloat16)
            attended = attended + lax.optimization_barrier(partial_value).astype(jnp.float32)
        centred = attended - lax.optimization_barrier(jnp.mean(attended, axis=1, keepdims=True))
        normed = centred * lax.rsqrt(lax.optimization_barrier(jnp.mean(centred * centred, axis=1, keepdims=True)) + 1e-05)
        mixed = (normed * gate).astype(jnp.bfloat16)
        result = (chosen.astype(jnp.float32) + jnp.dot(mixed, out_weight, preferred_element_type=jnp.float32)).astype(jnp.bfloat16)
        return (result, picked)
    results, indices = lax.map(per_user, jnp.arange(USERS, dtype=jnp.int32))
    ranked = jnp.zeros((CANDS, feature_width), jnp.bfloat16)
    ranked = ranked.at[indices.reshape(-1)].set(results.reshape(-1, feature_width), mode='drop')
    return ranked
```

```python
import functools

import jax
import jax.numpy as jnp
from jax import lax
from jax.experimental import pallas as pl
from jax.experimental.pallas import tpu as pltpu
from jax.sharding import PartitionSpec as P

HEADS = 8
CAP = 8
FOLD = 2
PIECE = CAP * FOLD
RING = 4
CHUNKS = 4
EVENT_BLOCK = 1024
MESH = pl.DeviceIdType.MESH
F32 = jnp.float32
BF16 = jnp.bfloat16


def dot(a, b):
    return jnp.dot(a, b, preferred_element_type=F32)


def layer_kernel(
    owners,
    length_ref, cand_ref, route_ref, wq_hbm, wg_hbm, wo_hbm, k_hbm, v_hbm,
    out_ref,
    keys, raw, vt, wq, wg, wo, fold, xc, part, pf, gl, gr, rl, rr, tot, ret, gate,
    load_sem, in_send, in_recv, x_send, x_recv, p_send, gl_recv, gr_recv, rl_recv, rr_recv,
    r_send, r_recv,
):
    me = lax.axis_index("owner")
    seq = lax.axis_index("seq")
    right, left = lax.rem(seq + 1, RING), lax.rem(seq + RING - 1, RING)
    per = owners // 4
    rows, width = cand_ref.shape
    half = width // FOLD
    head = width // HEADS
    events = keys.shape[0]
    block = min(EVENT_BLOCK, events)
    span = per * CAP

    loads = [
        pltpu.make_async_copy(src, dst, load_sem.at[i])
        for i, (src, dst) in enumerate(
            [(wq_hbm, wq), (v_hbm.at[0], raw), (wg_hbm, wg), (k_hbm.at[0], keys), (wo_hbm, wo)]
        )
    ]
    load_wq, load_v, load_wg, load_k, load_wo = loads
    for load in loads:
        load.start()

    barrier = pltpu.get_barrier_semaphore()

    def greet(i, carry):
        other = lax.rem(me + i, owners)
        pl.semaphore_signal(barrier, inc=1, device_id=(other, seq), device_id_type=MESH)
        return carry

    lax.fori_loop(1, owners, greet, 0)
    for other in (left, right):
        pl.semaphore_signal(barrier, inc=1, device_id=(me, other), device_id_type=MESH)

    def remote(src, dst, send, recv, owner, place):
        return pltpu.make_async_remote_copy(
            src_ref=src, dst_ref=dst, send_sem=send, recv_sem=recv,
            device_id=(owner, place), device_id_type=MESH,
        )

    def await_bytes(ref, sem):
        pltpu.make_async_copy(ref, ref, sem).wait()

    route_lane = jnp.broadcast_to(route_ref[...].astype(F32), (rows, rows))
    route_row = jnp.transpose(route_lane)
    lane = lax.broadcasted_iota(jnp.int32, (rows, rows), 1)
    sub = lax.broadcasted_iota(jnp.int32, (rows, rows), 0)
    same = route_lane == route_row
    before = jnp.sum(jnp.where(same & (sub < lane), 1.0, 0.0), axis=0, keepdims=True)
    place_lane = (route_ref[...].astype(F32) * PIECE + before).astype(jnp.int32)
    slot = lax.broadcasted_iota(jnp.int32, (owners * PIECE, rows), 0)

    load_wq.wait()
    scale = 0.5 * head ** (-0.5)
    query = (dot(cand_ref[...], wq[...]) * scale).astype(BF16)
    packed = sum(
        dot(
            jnp.where(slot == place_lane + CAP * f, 1.0, 0.0).astype(BF16),
            query[:, f * half:(f + 1) * half],
        )
        for f in range(FOLD)
    )
    fold[...] = packed.astype(BF16)

    pl.semaphore_wait(barrier, owners + 1)

    quarter = me // per
    spot = pl.ds(pl.multiple_of(lax.rem(me, per) * PIECE, PIECE), PIECE)
    home = xc.at[3 * lax.rem(quarter, 2), quarter // 2, spot, :]

    def piece(ref, owner):
        return ref.at[pl.ds(pl.multiple_of(owner * PIECE, PIECE), PIECE), :]

    def scatter(i, carry):
        other = lax.rem(me + i, owners)
        remote(piece(fold, other), home, in_send.at[0], in_recv.at[quarter], other, seq).start()
        return carry

    lax.fori_loop(1, owners, scatter, 0)
    pltpu.make_async_copy(piece(fold, me), home, in_recv.at[quarter]).start()

    load_wg.wait()
    gated = dot(cand_ref[...], wg[...])
    gate[...] = gated / (1.0 + jnp.exp(-gated))

    load_v.wait()
    limit = length_ref[0] - seq * events

    def turn(i, carry):
        at = pl.ds(pl.multiple_of(i * block, block), block)
        event = i * block + lax.broadcasted_iota(jnp.int32, (block, head), 0)
        for h in range(HEADS):
            cols = slice(h * head, (h + 1) * head)
            values = jnp.where(event < limit, raw[at, cols].astype(F32), 0.0)
            vt[cols, at] = jnp.transpose(values).astype(BF16)
        return carry

    turns = events // block
    lax.fori_loop(0, turns // 2, turn, 0)

    own = {0: (0, 0), 2: (0, 1), 1: (3, 0), 3: (3, 1)}
    to_right = {0: (0, 2), 1: (1, 0), 2: (2, 0), 3: (3, 2)}
    to_left = {2: (0, 3), 3: (1, 1), 0: (2, 1), 1: (3, 3)}

    def pass_on(source, dest, send, place):
        c, j = dest
        remote(
            xc.at[source[0], source[1]], xc.at[c, j], x_send.at[send], x_recv.at[c * 4 + j],
            me, place,
        ).start()

    def await_block(c, j):
        await_bytes(xc.at[c, j], x_recv.at[c * 4 + j])

    for rq, lq in ((0, 2), (1, 3)):
        for q in (rq, lq):
            await_bytes(xc.at[own[q][0], own[q][1]], in_recv.at[q])
        pass_on(own[rq], to_right[rq], rq, right)
        pass_on(own[lq], to_left[lq], 6 + lq, left)

    lax.fori_loop(turns // 2, turns, turn, 0)
    load_k.wait()

    def before_chunk(c):
        if c == 0:
            await_block(0, 2)
            await_block(0, 3)
            pass_on((0, 2), (1, 2), 4, right)
            pass_on((0, 3), (1, 3), 10, left)
            for rq, lq in ((2, 0), (3, 1)):
                pass_on(own[rq], to_right[rq], rq, right)
                pass_on(own[lq], to_left[lq], 6 + lq, left)
        if c == 1:
            for j in range(4):
                await_block(1, j)
            pass_on((1, 0), (2, 2), 5, right)
            pass_on((1, 1), (2, 3), 11, left)
        if c == 2:
            for j in range(4):
                await_block(2, j)
        if c == 3:
            await_block(3, 2)
            await_block(3, 3)

    def give(c, j, dest, recv, send, place):
        remote(part.at[c, j], dest, p_send.at[send], recv, me, place).start()

    def add(c, j, ref, at, sem):
        await_bytes(ref.at[at], sem.at[at])
        part[c, j] = (part[c, j].astype(F32) + ref[at].astype(F32)).astype(BF16)

    def after_chunk(c):
        if c == 0:
            give(0, 3, gl.at[2], gl_recv.at[2], 0, right)
            give(0, 2, gr.at[0], gr_recv.at[0], 6, left)
        if c == 1:
            give(1, 2, rl.at[0], rl_recv.at[0], 1, right)
            give(1, 3, rr.at[0], rr_recv.at[0], 7, left)
            give(1, 1, gl.at[3], gl_recv.at[3], 2, right)
            give(1, 0, gr.at[1], gr_recv.at[1], 8, left)
        if c == 2:
            give(2, 2, rl.at[1], rl_recv.at[1], 3, right)
            give(2, 3, rr.at[1], rr_recv.at[1], 9, left)
            add(2, 1, rl, 0, rl_recv)
            give(2, 1, gl.at[0], gl_recv.at[0], 4, right)
            add(2, 0, rr, 0, rr_recv)
            give(2, 0, gr.at[2], gr_recv.at[2], 10, left)
        if c == 3:
            add(3, 3, rl, 1, rl_recv)
            give(3, 3, gl.at[1], gl_recv.at[1], 5, right)
            add(3, 2, rr, 1, rr_recv)
            give(3, 2, gr.at[3], gr_recv.at[3], 11, left)

    def attend(c):
        def columns(h):
            f, cols = h // (HEADS // FOLD), slice(h % (HEADS // FOLD) * head, (h % (HEADS // FOLD) + 1) * head)
            parts = [
                xc[c, j, :, cols].astype(F32).reshape(per, FOLD, CAP, head)[:, f].reshape(span, head)
                for j in range(4)
            ]
            return jnp.transpose(jnp.concatenate(parts, axis=0)).astype(BF16)

        def weigh(h, e, turned):
            score = dot(keys[e * block:(e + 1) * block, h * head:(h + 1) * head], turned)
            return (score + score * jnp.tanh(score)).astype(BF16)

        def finish(h, total):
            f, cols = h // (HEADS // FOLD), slice(h % (HEADS // FOLD) * head, (h % (HEADS // FOLD) + 1) * head)
            back = jnp.transpose(total)
            for j in range(4):
                pf[j, :, f, :, cols] = back[j * span:(j + 1) * span].reshape(per, CAP, head)

        waiting = None
        totals = {}

        def settle(h, e, weight):
            term = dot(vt[h * head:(h + 1) * head, e * block:(e + 1) * block], weight)
            totals[h] = totals[h] + term if e else term
            if e == events // block - 1:
                finish(h, totals.pop(h))

        for h in range(HEADS):
            turned = columns(h)
            for e in range(events // block):
                weight = weigh(h, e, turned)
                if waiting is not None:
                    settle(*waiting)
                waiting = (h, e, weight)
        settle(*waiting)
        for j in range(4):
            part[c, j] = pf[j].reshape(per * PIECE, half).astype(BF16)

    def step(c, carry):
        for now in range(CHUNKS):
            pl.when(c == now)(functools.partial(before_chunk, now))
        attend(c)
        for now in range(CHUNKS):
            pl.when(c == now)(functools.partial(after_chunk, now))
        return carry

    lax.fori_loop(0, CHUNKS, step, 0)

    landing = piece(ret, me)
    for q in (0, 2, 1, 3):
        await_bytes(gl.at[q], gl_recv.at[q])
        await_bytes(gr.at[q], gr_recv.at[q])
        mine = part[own[q][0], own[q][1]].astype(F32)
        tot[q] = (mine + gl[q].astype(F32) + gr[q].astype(F32)).astype(BF16)

        def hand_back(i, carry, q=q):
            spot = lax.rem(me + i, per)
            other = q * per + spot
            source = tot.at[q, pl.ds(pl.multiple_of(spot * PIECE, PIECE), PIECE), :]

            @pl.when(other == me)
            def _():
                pltpu.make_async_copy(source, landing, r_recv.at[0]).start()

            @pl.when(other != me)
            def _():
                remote(source, landing, r_send.at[0], r_recv.at[0], other, seq).start()

            return carry

        lax.fori_loop(0, per, hand_back, 0)

    place_row = jnp.transpose(
        jnp.broadcast_to(place_lane.astype(F32), (rows, rows))
    ).astype(jnp.int32)[:, :1]
    slot_lane = lax.broadcasted_iota(jnp.int32, (rows, owners * PIECE), 1)
    picks = [
        jnp.where(slot_lane == place_row + CAP * f, 1.0, 0.0).astype(BF16) for f in range(FOLD)
    ]
    load_wo.wait()

    await_bytes(ret, r_recv.at[0])
    attended = jnp.concatenate([dot(pick, ret[...]) for pick in picks], axis=1)
    centred = attended - jnp.mean(attended, axis=1, keepdims=True)
    normed = centred * lax.rsqrt(jnp.mean(centred * centred, axis=1, keepdims=True) + 1e-05)
    mixed = (normed * gate[...]).astype(BF16)
    out_ref[...] = (cand_ref[...].astype(F32) + dot(mixed, wo[...])).astype(BF16)

    sent = (owners - 1) * PIECE
    await_bytes(fold.at[pl.ds(0, sent), :], in_send.at[0])
    await_bytes(ret.at[pl.ds(0, sent), :], r_send.at[0])
    for i in range(12):
        await_bytes(xc.at[0, 0], x_send.at[i])
        await_bytes(part.at[0, 0], p_send.at[i])


def body(cand, route, lengths, keys, values, wq, wg, wo):
    owners = lax.axis_size("owner")
    rows, width = cand.shape
    events = keys.shape[1]
    half = width // FOLD
    per = owners // 4
    square = pltpu.VMEM((width, width), BF16)
    slots = pltpu.VMEM((owners * PIECE, half), BF16)
    blocks = lambda *lead: pltpu.VMEM((*lead, per * PIECE, half), BF16)
    sems = lambda n: pltpu.SemaphoreType.DMA((n,))
    vmem = pl.BlockSpec(memory_space=pltpu.VMEM)
    hbm = pl.BlockSpec(memory_space=pl.ANY)
    return pl.pallas_call(
        functools.partial(layer_kernel, owners),
        out_shape=jax.ShapeDtypeStruct((rows, width), BF16),
        in_specs=[pl.BlockSpec(memory_space=pltpu.SMEM), vmem, vmem, hbm, hbm, hbm, hbm, hbm],
        out_specs=vmem,
        scratch_shapes=[
            pltpu.VMEM((events, width), BF16),
            pltpu.VMEM((events, width), BF16),
            pltpu.VMEM((width, events), BF16),
            square, square, square,
            slots,
            blocks(CHUNKS, 4),
            blocks(CHUNKS, 4),
            pltpu.VMEM((4, per, FOLD, CAP, half), F32),
            blocks(4), blocks(4), blocks(2), blocks(2), blocks(4),
            slots,
            pltpu.VMEM((rows, width), F32),
            sems(5), sems(1), sems(4), sems(12), sems(16), sems(12),
            sems(4), sems(4), sems(2), sems(2), sems(1), sems(1),
        ],
        compiler_params=pltpu.CompilerParams(
            collective_id=0, has_side_effects=True, vmem_limit_bytes=56 * 2**20
        ),
        name="candidate_layer",
    )(lengths, cand, route.reshape(1, rows), wq, wg, wo, keys, values)


def solution(mesh):
    placed = (
        P(("owner", "seq"), None),
        P(("owner", "seq")),
        P("owner"),
        P("owner", "seq", None),
        P("owner", "seq", None),
        P(),
        P(),
        P(),
    )
    return jax.shard_map(
        body, mesh=mesh, in_specs=placed, out_specs=P(("owner", "seq"), None), check_vma=False
    )
```

```python
import functools

import jax
import jax.numpy as jnp
from jax import lax
from jax.experimental import pallas as pl
from jax.experimental.pallas import tpu as pltpu
from jax.sharding import PartitionSpec as P

HEADS = 8
CAP = 8
FOLD = 2
PIECE = CAP * FOLD
RING = 4
GROUPS = HEADS // FOLD
RAW = 2
OWN, NEAR, FAR, REST = range(RING)
EVENT_BLOCK = 1024
MESH = pl.DeviceIdType.MESH
F32 = jnp.float32
BF16 = jnp.bfloat16


def dot(a, b):
    return jnp.dot(a, b, preferred_element_type=F32)


def layer_kernel(
    owners,
    length_ref, cand_ref, route_ref, wq_hbm, wg_hbm, wo_hbm, k_hbm, v_hbm,
    out_ref,
    keys, raw, vt, wq, wg, wo, fold, wide, rawq, seats, xc, part, pf, late, sums, gl, gr, rl, rr, tot, ret,
    gate,
    load_sem, in_send, in_recv, w_send, w_recv, x_send, x_recv, p_send, p_recv, r_send, r_recv,
):
    me = lax.axis_index("owner")
    seq = lax.axis_index("seq")
    right, left = lax.rem(seq + 1, RING), lax.rem(seq + RING - 1, RING)
    per = owners // 4
    rows, width = cand_ref.shape
    head = width // HEADS
    events = keys.shape[0]
    block = min(EVENT_BLOCK, events)
    blocks = events // block
    span = per * CAP

    half = width // FOLD
    lead = [(slice(None), slice(f * half, f * half + head)) for f in range(FOLD)]
    rest = [(slice(None), slice(f * half + head, (f + 1) * half)) for f in range(FOLD)]
    loads = [
        pltpu.make_async_copy(src, dst, load_sem.at[i])
        for i, (src, dst) in enumerate(
            [(wq_hbm.at[part_of], wq.at[part_of]) for part_of in lead + rest]
            + [(v_hbm.at[0], raw), (wg_hbm, wg), (k_hbm.at[0], keys), (wo_hbm, wo)]
        )
    ]
    load_wq, (load_v, load_wg, load_k, load_wo) = loads[:2 * FOLD], loads[2 * FOLD:]
    for load in loads:
        load.start()

    barrier = pltpu.get_barrier_semaphore()

    def greet(i, carry):
        other = lax.rem(me + i, owners)
        pl.semaphore_signal(barrier, inc=1, device_id=(other, seq), device_id_type=MESH)
        return carry

    lax.fori_loop(1, owners, greet, 0)
    for other in (left, right):
        pl.semaphore_signal(barrier, inc=1, device_id=(me, other), device_id_type=MESH)

    def remote(src, dst, send, recv, owner, place):
        return pltpu.make_async_remote_copy(
            src_ref=src, dst_ref=dst, send_sem=send, recv_sem=recv,
            device_id=(owner, place), device_id_type=MESH,
        )

    def await_bytes(ref, sem):
        pltpu.make_async_copy(ref, ref, sem).wait()

    route_lane = jnp.broadcast_to(route_ref[...].astype(F32), (rows, rows))
    route_row = jnp.transpose(route_lane)
    lane = lax.broadcasted_iota(jnp.int32, (rows, rows), 1)
    sub = lax.broadcasted_iota(jnp.int32, (rows, rows), 0)
    same = route_lane == route_row
    before = jnp.sum(jnp.where(same & (sub < lane), 1.0, 0.0), axis=0, keepdims=True)
    place_lane = (route_ref[...].astype(F32) * PIECE + before).astype(jnp.int32)
    slot = lax.broadcasted_iota(jnp.int32, (owners * PIECE, rows), 0)

    scale = 0.5 * head ** (-0.5)

    def project(f, low, high):
        at = slice(f * half + low * head, f * half + high * head)
        return (dot(cand_ref[...], wq[:, at]) * scale).astype(BF16)

    def pack(places, queries):
        return sum(
            dot(jnp.where(slot == places + CAP * f, 1.0, 0.0).astype(BF16), queries[f])
            for f in range(FOLD)
        ).astype(BF16)

    for load in load_wq[:FOLD]:
        load.wait()
    fold[0] = pack(place_lane, [project(f, 0, 1) for f in range(FOLD)])

    pl.semaphore_wait(barrier, owners + 1)

    def piece(ref, g, owner):
        return ref.at[g, pl.ds(pl.multiple_of(owner * PIECE, PIECE), PIECE), :]

    def scatter(g):
        home = xc.at[g, me, seq]

        def send(i, carry):
            other = lax.rem(me + i, owners)
            remote(piece(fold, g, other), home, in_send.at[g], in_recv.at[g], other, seq).start()
            return carry

        lax.fori_loop(1, owners, send, 0)
        pltpu.make_async_copy(piece(fold, g, me), home, in_recv.at[g]).start()

    def await_own(g):
        await_bytes(xc.at[g, :, 0], in_recv.at[g])

    def pass_raw(kind, ref, place):
        remote(ref, ref, w_send.at[kind], w_recv.at[kind], me, place).start()

    def raw_near():
        pass_raw(0, rawq.at[seq], right)
        pass_raw(1, rawq.at[seq], left)
        pass_raw(2, seats.at[seq], right)
        pass_raw(3, seats.at[seq], left)

    lower, upper = pl.ds(0, rows // 2), pl.ds(rows // 2, rows // 2)

    def raw_far():
        for kind in range(2):
            await_bytes(rawq.at[0], w_recv.at[kind])
        for kind in range(2, 4):
            await_bytes(seats.at[0], w_recv.at[kind])
        pass_raw(4, rawq.at[left, lower], right)
        pass_raw(5, rawq.at[right, upper], left)
        pass_raw(6, seats.at[left], right)

    def scatter_raw():
        for kind in range(4, 6):
            await_bytes(rawq.at[0, lower], w_recv.at[kind])
        await_bytes(seats.at[0], w_recv.at[6])
        for s in range(RING):
            queries = [rawq[s, :, f * head:(f + 1) * head] for f in range(FOLD)]
            packed = pack(seats[s, 0:1, :].astype(jnp.int32), queries)
            wide[:, s] = packed.reshape(owners, PIECE, head)

        def send(i, carry):
            other = lax.rem(me + i, owners)
            remote(
                wide.at[other], xc.at[RAW, me], in_send.at[RAW], in_recv.at[RAW], other, seq
            ).start()
            return carry

        lax.fori_loop(1, owners, send, 0)
        pltpu.make_async_copy(wide.at[me], xc.at[RAW, me], in_recv.at[RAW]).start()

    def await_raw():
        await_bytes(xc.at[RAW], in_recv.at[RAW])

    first, last = pl.ds(0, 2), pl.ds(2, 2)
    low, high = pl.ds(0, owners // 2), pl.ds(owners // 2, owners // 2)

    def pass_on(g, kind, which, source, place):
        ref = xc.at[g, which, source]
        remote(
            ref, ref, x_send.at[g * 6 + kind], x_recv.at[g * 6 + kind], me, place
        ).start()

    def pass_near(g):
        pass_on(g, 0, low, seq, right)
        pass_on(g, 1, high, seq, left)

    def pass_rest(g):
        pass_on(g, 4, high, seq, right)
        pass_on(g, 5, low, seq, left)

    def pass_far(g):
        pass_on(g, 2, low, left, right)
        pass_on(g, 3, high, right, left)

    def await_pair(g, kind):
        await_bytes(xc.at[g, low, 0], x_recv.at[g * 6 + kind])

    def await_near(g):
        await_pair(g, 0)
        await_pair(g, 1)

    def await_far(g):
        await_pair(g, 2)
        await_pair(g, 3)

    def await_rest(g):
        await_pair(g, 4)
        await_pair(g, 5)

    def give(g, kind, source, pair, dest, place):
        remote(
            part.at[g, source, pair], dest, p_send.at[g * 6 + kind], p_recv.at[g * 6 + kind],
            me, place,
        ).start()

    def give_near(g):
        give(g, 0, NEAR, last, gl.at[g, last], right)
        give(g, 1, NEAR, first, gr.at[g, first], left)

    def give_far(g):
        give(g, 2, FAR, first, rl.at[g], right)
        give(g, 3, FAR, last, rr.at[g], left)

    def await_part(g, kind):
        await_bytes(rl.at[g], p_recv.at[g * 6 + kind])

    def give_rest(g):
        await_part(g, 2)
        part[g, REST, 0:2] = (part[g, REST, 0:2].astype(F32) + rl[g].astype(F32)).astype(BF16)
        give(g, 4, REST, first, gl.at[g, first], right)
        await_part(g, 3)
        part[g, REST, 2:4] = (part[g, REST, 2:4].astype(F32) + rr[g].astype(F32)).astype(BF16)
        give(g, 5, REST, last, gr.at[g, last], left)

    def hand_back(pair):
        for g in (2 * pair, 2 * pair + 1):
            for kind in (0, 1, 4, 5):
                await_part(g, kind)
            total = part[g, OWN].astype(F32) + gl[g].astype(F32) + gr[g].astype(F32)
            at = slice(g % 2 * head, (g % 2 + 1) * head)
            tot[pair, :, at] = total.astype(BF16).reshape(owners * PIECE, head)
        landing = piece(ret, pair, me)

        def send(i, carry):
            other = lax.rem(me + i, owners)
            remote(
                piece(tot, pair, other), landing, r_send.at[pair], r_recv.at[pair], other, seq
            ).start()
            return carry

        lax.fori_loop(1, owners, send, 0)
        pltpu.make_async_copy(piece(tot, pair, me), landing, r_recv.at[pair]).start()

    def turn(g):
        limit = length_ref[0] - seq * events

        def some(i, carry):
            at = pl.ds(pl.multiple_of(i * block, block), block)
            event = i * block + lax.broadcasted_iota(jnp.int32, (block, head), 0)
            for f in range(FOLD):
                cols = slice((f * GROUPS + g) * head, (f * GROUPS + g + 1) * head)
                values = jnp.where(event < limit, raw[at, cols].astype(F32), 0.0)
                vt[cols, at] = jnp.transpose(values).astype(BF16)
            return carry

        lax.fori_loop(0, blocks, some, 0)

    def unit(n):
        early = 1 - n // 8
        step, turned = lax.rem(n, 4), lax.div(jnp.maximum(n, 8) - 8, 2)
        early_chunk = step + step // 2 * (1 - 2 * lax.rem(step, 2))
        late_chunk = 2 + turned - 3 * (turned // 2) - 2 * (turned // 3)
        return (
            early * (n // 4) + (1 - early) * (2 + lax.rem(n, 2)),
            early * early_chunk + (1 - early) * late_chunk,
        )

    def cols(g, f):
        return pl.ds(pl.multiple_of((f * GROUPS + g) * head, head), head)

    def finish(f, total):
        back = jnp.transpose(total)
        for j in range(4):
            pf[j, :, f] = back[j * span:(j + 1) * span].reshape(per, CAP, head)

    def settle(g, f, e, weight):
        return dot(vt[cols(g, f), e * block:(e + 1) * block], weight)

    def settle_late(g, c):
        finish(FOLD - 1, sums[...] + settle(g, FOLD - 1, blocks - 1, late[...]))
        part[g, c] = pf[...].reshape(4, per * PIECE, head).astype(BF16)

    def attend(n):
        g, c = unit(n)

        before, after = lax.rem(seq - c + RING, RING), lax.rem(seq + c, RING)

        def columns(f):
            parts = [
                xc[g, which, s].astype(F32).reshape(-1, FOLD, CAP, head)[:, f].reshape(-1, head)
                for which, s in ((low, before), (high, after))
            ]
            return jnp.transpose(jnp.concatenate(parts, axis=0)).astype(BF16)

        def weigh(f, e, turned):
            score = dot(keys[e * block:(e + 1) * block, cols(g, f)], turned)
            return (score + score * jnp.tanh(score)).astype(BF16)

        turned = [columns(f) for f in range(FOLD)]
        waiting = None
        total = None
        for f in range(FOLD):
            for e in range(blocks):
                weight = weigh(f, e, turned[f])
                if waiting is None:
                    settle_late(*unit(jnp.maximum(n - 1, 0)))
                else:
                    term = settle(g, *waiting)
                    total = term if waiting[1] == 0 else total + term
                    if waiting[1] == blocks - 1:
                        finish(waiting[0], total)
                waiting = (f, e, weight)
        sums[...] = total
        late[...] = waiting[2]

    def run(count, after):
        def step(n, carry):
            attend(n)
            def pick(acts, start, stop):
                if stop - start == 1:
                    for act, *args in acts[start]:
                        act(*args)
                    return
                mid = (start + stop) // 2
                for test, lo, hi in ((n < mid, start, mid), (n >= mid, mid, stop)):
                    some = {k: v for k, v in acts.items() if lo <= k < hi}
                    if some:
                        pl.when(test)(functools.partial(pick, some, lo, hi))

            pick(after, 0, count)
            return carry

        lax.fori_loop(0, count, step, 0)

    def gates():
        load_wg.wait()
        gated = dot(cand_ref[...], wg[...])
        gate[...] = gated / (1.0 + jnp.exp(-gated))

    scatter(0)
    for load in load_wq[FOLD:]:
        load.wait()
    others = [project(f, 1, GROUPS) for f in range(FOLD)]
    for f in range(FOLD):
        rawq[seq, :, f * head:(f + 1) * head] = others[f][:, (RAW - 1) * head:RAW * head]
    seats[seq] = jnp.broadcast_to(place_lane.astype(F32), (8, rows))
    raw_near()
    packed = pack(place_lane, others)
    for g in range(1, GROUPS):
        if g != RAW:
            fold[g] = packed[:, (g - 1) * head:g * head]
            scatter(g)
    late[...] = jnp.zeros_like(late)
    sums[...] = jnp.zeros_like(sums)
    load_v.wait()
    turn(0)
    turn(1)
    gates()
    await_own(0)
    pass_near(0)
    pass_rest(0)
    load_k.wait()
    run(4 * GROUPS, {
        0: [
            (await_own, 1), (pass_near, 1), (raw_far,), (turn, 2), (await_near, 0),
            (pass_far, 0), (pass_rest, 1),
        ],
        1: [(await_rest, 0), (await_own, 3), (pass_near, 3), (turn, 3)],
        2: [
            (give_near, 0), (await_near, 1), (pass_far, 1), (scatter_raw,), (await_far, 0),
            (pass_rest, 3),
        ],
        4: [(give_far, 0), (await_near, 3), (pass_far, 3)],
        5: [(await_rest, 1)],
        6: [(give_near, 1), (await_far, 1)],
        7: [(give_rest, 0), (await_raw,)],
        8: [(give_far, 1), (await_far, 3)],
        9: [(give_far, 2)],
        10: [(give_far, 3), (await_rest, 3)],
        11: [(give_rest, 1)],
        12: [(give_rest, 2)],
        13: [(give_near, 2), (give_rest, 3)],
        14: [(give_near, 3), (hand_back, 0)],
    })
    settle_late(*unit(4 * GROUPS - 1))
    hand_back(1)

    place_row = jnp.transpose(
        jnp.broadcast_to(place_lane.astype(F32), (rows, rows))
    ).astype(jnp.int32)[:, :1]
    slot_lane = lax.broadcasted_iota(jnp.int32, (rows, owners * PIECE), 1)
    picks = [
        jnp.where(slot_lane == place_row + CAP * f, 1.0, 0.0).astype(BF16) for f in range(FOLD)
    ]
    load_wo.wait()

    for pair in range(GROUPS // 2):
        await_bytes(ret.at[pair], r_recv.at[pair])
    attended = jnp.concatenate(
        [dot(pick, ret[pair]) for pick in picks for pair in range(GROUPS // 2)], axis=1
    )
    centred = attended - jnp.mean(attended, axis=1, keepdims=True)
    normed = centred * lax.rsqrt(jnp.mean(centred * centred, axis=1, keepdims=True) + 1e-05)
    mixed = (normed * gate[...]).astype(BF16)
    out_ref[...] = dot(mixed, wo[...])

    sent = pl.ds(0, (owners - 1) * PIECE)
    for pair in range(GROUPS // 2):
        await_bytes(tot.at[pair, sent], r_send.at[pair])
    await_bytes(wide.at[pl.ds(0, owners - 1)], in_send.at[RAW])
    for kind in range(2):
        await_bytes(rawq.at[0], w_send.at[kind])
    for kind in range(4, 6):
        await_bytes(rawq.at[0, lower], w_send.at[kind])
    for kind in (2, 3, 6):
        await_bytes(seats.at[0], w_send.at[kind])
    for g in range(GROUPS):
        for kind in range(6):
            await_bytes(part.at[g, OWN, first], p_send.at[g * 6 + kind])
            if g != RAW:
                await_bytes(xc.at[g, low, 0], x_send.at[g * 6 + kind])
        if g != RAW:
            await_bytes(fold.at[g, sent], in_send.at[g])


def body(cand, route, lengths, keys, values, wq, wg, wo):
    owners = lax.axis_size("owner")
    rows, width = cand.shape
    head = width // HEADS
    events = keys.shape[1]
    per = owners // 4
    square = pltpu.VMEM((width, width), BF16)
    slots = pltpu.VMEM((GROUPS, owners * PIECE, head), BF16)
    pairs = pltpu.VMEM((GROUPS // 2, owners * PIECE, 2 * head), BF16)
    blocks = lambda *lead: pltpu.VMEM((GROUPS, *lead, per * PIECE, head), BF16)
    sems = lambda n: pltpu.SemaphoreType.DMA((n,))
    vmem = pl.BlockSpec(memory_space=pltpu.VMEM)
    hbm = pl.BlockSpec(memory_space=pl.ANY)
    change = pl.pallas_call(
        functools.partial(layer_kernel, owners),
        out_shape=jax.ShapeDtypeStruct((rows, width), F32),
        in_specs=[pl.BlockSpec(memory_space=pltpu.SMEM), vmem, vmem, hbm, hbm, hbm, hbm, hbm],
        out_specs=vmem,
        scratch_shapes=[
            pltpu.VMEM((events, width), BF16),
            pltpu.VMEM((events, width), BF16),
            pltpu.VMEM((width, events), BF16),
            square, square, square,
            slots,
            pltpu.VMEM((owners, RING, PIECE, head), BF16),
            pltpu.VMEM((RING, rows, FOLD * head), BF16),
            pltpu.VMEM((RING, 8, rows), F32),
            pltpu.VMEM((GROUPS, owners, RING, PIECE, head), BF16),
            blocks(4, 4),
            pltpu.VMEM((4, per, FOLD, CAP, head), F32),
            pltpu.VMEM((min(EVENT_BLOCK, events), 4 * per * CAP), BF16),
            pltpu.VMEM((head, 4 * per * CAP), F32),
            blocks(4), blocks(4), blocks(2), blocks(2),
            pairs,
            pairs,
            pltpu.VMEM((rows, width), F32),
            sems(8), sems(GROUPS), sems(GROUPS), sems(7), sems(7), sems(6 * GROUPS), sems(6 * GROUPS),
            sems(6 * GROUPS), sems(6 * GROUPS), sems(2), sems(2),
        ],
        compiler_params=pltpu.CompilerParams(
            collective_id=0, has_side_effects=True, vmem_limit_bytes=56 * 2**20
        ),
        name="candidate_layer",
    )(lengths, cand, route.reshape(1, rows), wq, wg, wo, keys, values)
    return (cand.astype(F32) + change).astype(BF16)


def solution(mesh):
    placed = (
        P(("owner", "seq"), None),
        P(("owner", "seq")),
        P("owner"),
        P("owner", "seq", None),
        P("owner", "seq", None),
        P(),
        P(),
        P(),
    )
    return jax.shard_map(
        body, mesh=mesh, in_specs=placed, out_specs=P(("owner", "seq"), None), check_vma=False
    )
```

```python
import functools

import jax
import jax.numpy as jnp
from jax import lax
from jax.experimental import pallas as pl
from jax.experimental.pallas import tpu as pltpu
from jax.sharding import PartitionSpec as P

HEADS = 8
CAP = 8
FOLD = 2
PIECE = CAP * FOLD
RING = 4
GROUPS = HEADS // FOLD
RAW = 2
OWN, NEAR, FAR, REST = range(RING)
EVENT_BLOCK = 1024
MESH = pl.DeviceIdType.MESH
F32 = jnp.float32
BF16 = jnp.bfloat16


def dot(a, b):
    return jnp.dot(a, b, preferred_element_type=F32)


def layer_kernel(
    owners,
    length_ref, cand_ref, route_ref, wq_hbm, wg_hbm, wo_hbm, k_hbm, v_hbm,
    out_ref,
    keys, raw, vt, wq, wg, wo, fold, wide, rawq, seats, xc, part, pf, late, sums, gl, gr, rl, rr, tot, ret,
    gate,
    load_sem, in_send, in_recv, w_send, w_recv, x_send, x_recv, p_send, p_recv, r_send, r_recv,
):
    me = lax.axis_index("owner")
    seq = lax.axis_index("seq")
    right, left = lax.rem(seq + 1, RING), lax.rem(seq + RING - 1, RING)
    per = owners // 4
    rows, width = cand_ref.shape
    head = width // HEADS
    events = keys.shape[0]
    block = min(EVENT_BLOCK, events)
    blocks = events // block
    span = per * CAP

    half = width // FOLD
    lead = [(slice(None), slice(f * half, f * half + head)) for f in range(FOLD)]
    rest = [(slice(None), slice(f * half + head, (f + 1) * half)) for f in range(FOLD)]
    loads = [
        pltpu.make_async_copy(src, dst, load_sem.at[i])
        for i, (src, dst) in enumerate(
            [(wq_hbm.at[part_of], wq.at[part_of]) for part_of in lead + rest]
            + [(v_hbm.at[0], raw), (wg_hbm, wg), (k_hbm.at[0], keys), (wo_hbm, wo)]
        )
    ]
    load_wq, (load_v, load_wg, load_k, load_wo) = loads[:2 * FOLD], loads[2 * FOLD:]
    for load in loads:
        load.start()

    barrier = pltpu.get_barrier_semaphore()

    def greet(i, carry):
        other = lax.rem(me + i, owners)
        pl.semaphore_signal(barrier, inc=1, device_id=(other, seq), device_id_type=MESH)
        return carry

    lax.fori_loop(1, owners, greet, 0)
    for other in (left, right):
        pl.semaphore_signal(barrier, inc=1, device_id=(me, other), device_id_type=MESH)

    def remote(src, dst, send, recv, owner, place):
        return pltpu.make_async_remote_copy(
            src_ref=src, dst_ref=dst, send_sem=send, recv_sem=recv,
            device_id=(owner, place), device_id_type=MESH,
        )

    def await_bytes(ref, sem):
        pltpu.make_async_copy(ref, ref, sem).wait()

    route_lane = jnp.broadcast_to(route_ref[...].astype(F32), (rows, rows))
    route_row = jnp.transpose(route_lane)
    lane = lax.broadcasted_iota(jnp.int32, (rows, rows), 1)
    sub = lax.broadcasted_iota(jnp.int32, (rows, rows), 0)
    same = route_lane == route_row
    before = jnp.sum(jnp.where(same & (sub < lane), 1.0, 0.0), axis=0, keepdims=True)
    place_lane = (route_ref[...].astype(F32) * PIECE + before).astype(jnp.int32)
    slot = lax.broadcasted_iota(jnp.int32, (owners * PIECE, rows), 0)

    scale = 0.5 * head ** (-0.5)

    def project(f, low, high):
        at = slice(f * half + low * head, f * half + high * head)
        return (dot(cand_ref[...], wq[:, at]) * scale).astype(BF16)

    def pack(places, queries):
        return sum(
            dot(jnp.where(slot == places + CAP * f, 1.0, 0.0).astype(BF16), queries[f])
            for f in range(FOLD)
        ).astype(BF16)

    for load in load_wq[:FOLD]:
        load.wait()
    fold[0] = pack(place_lane, [project(f, 0, 1) for f in range(FOLD)])

    pl.semaphore_wait(barrier, owners + 1)

    def piece(ref, g, owner):
        return ref.at[g, pl.ds(pl.multiple_of(owner * PIECE, PIECE), PIECE), :]

    def scatter(g):
        home = xc.at[g, me, seq]

        def send(i, carry):
            other = lax.rem(me + i, owners)
            remote(piece(fold, g, other), home, in_send.at[g], in_recv.at[g], other, seq).start()
            return carry

        lax.fori_loop(1, owners, send, 0)
        pltpu.make_async_copy(piece(fold, g, me), home, in_recv.at[g]).start()

    def await_own(g):
        await_bytes(xc.at[g, :, 0], in_recv.at[g])

    def pass_raw(kind, ref, place):
        remote(ref, ref, w_send.at[kind], w_recv.at[kind], me, place).start()

    def raw_near():
        pass_raw(0, rawq.at[seq], right)
        pass_raw(1, rawq.at[seq], left)
        pass_raw(2, seats.at[seq], right)
        pass_raw(3, seats.at[seq], left)

    lower, upper = pl.ds(0, rows // 2), pl.ds(rows // 2, rows // 2)

    def raw_far():
        for kind in range(2):
            await_bytes(rawq.at[0], w_recv.at[kind])
        for kind in range(2, 4):
            await_bytes(seats.at[0], w_recv.at[kind])
        pass_raw(4, rawq.at[left, lower], right)
        pass_raw(5, rawq.at[right, upper], left)
        pass_raw(6, seats.at[left], right)

    def scatter_raw():
        for kind in range(4, 6):
            await_bytes(rawq.at[0, lower], w_recv.at[kind])
        await_bytes(seats.at[0], w_recv.at[6])
        for s in range(RING):
            queries = [rawq[s, :, f * head:(f + 1) * head] for f in range(FOLD)]
            packed = pack(seats[s, 0:1, :].astype(jnp.int32), queries)
            wide[:, s] = packed.reshape(owners, PIECE, head)

        def send(i, carry):
            other = lax.rem(me + i, owners)
            remote(
                wide.at[other], xc.at[RAW, me], in_send.at[RAW], in_recv.at[RAW], other, seq
            ).start()
            return carry

        lax.fori_loop(1, owners, send, 0)
        pltpu.make_async_copy(wide.at[me], xc.at[RAW, me], in_recv.at[RAW]).start()

    def await_raw():
        await_bytes(xc.at[RAW], in_recv.at[RAW])

    first, last = pl.ds(0, 2), pl.ds(2, 2)
    low, high = pl.ds(0, owners // 2), pl.ds(owners // 2, owners // 2)

    def pass_on(g, kind, which, source, place):
        ref = xc.at[g, which, source]
        remote(
            ref, ref, x_send.at[g * 6 + kind], x_recv.at[g * 6 + kind], me, place
        ).start()

    def pass_near(g):
        pass_on(g, 0, low, seq, right)
        pass_on(g, 1, high, seq, left)

    def pass_rest(g):
        pass_on(g, 4, high, seq, right)
        pass_on(g, 5, low, seq, left)

    def pass_far(g):
        pass_on(g, 2, low, left, right)
        pass_on(g, 3, high, right, left)

    def await_pair(g, kind):
        await_bytes(xc.at[g, low, 0], x_recv.at[g * 6 + kind])

    def await_near(g):
        await_pair(g, 0)
        await_pair(g, 1)

    def await_far(g):
        await_pair(g, 2)
        await_pair(g, 3)

    def await_rest(g):
        await_pair(g, 4)
        await_pair(g, 5)

    def give(g, kind, source, pair, dest, place):
        remote(
            part.at[g, source, pair], dest, p_send.at[g * 6 + kind], p_recv.at[g * 6 + kind],
            me, place,
        ).start()

    def give_near(g):
        give(g, 0, NEAR, last, gl.at[g, last], right)
        give(g, 1, NEAR, first, gr.at[g, first], left)

    def give_far(g):
        give(g, 2, FAR, first, rl.at[g], right)
        give(g, 3, FAR, last, rr.at[g], left)

    def await_part(g, kind):
        await_bytes(rl.at[g], p_recv.at[g * 6 + kind])

    def give_rest(g):
        await_part(g, 2)
        part[g, REST, 0:2] = (part[g, REST, 0:2].astype(F32) + rl[g].astype(F32)).astype(BF16)
        give(g, 4, REST, first, gl.at[g, first], right)
        await_part(g, 3)
        part[g, REST, 2:4] = (part[g, REST, 2:4].astype(F32) + rr[g].astype(F32)).astype(BF16)
        give(g, 5, REST, last, gr.at[g, last], left)

    def hand_back(pair):
        for g in (2 * pair, 2 * pair + 1):
            for kind in (0, 1, 4, 5):
                await_part(g, kind)
            total = part[g, OWN].astype(F32) + gl[g].astype(F32) + gr[g].astype(F32)
            at = slice(g % 2 * head, (g % 2 + 1) * head)
            tot[pair, :, at] = total.astype(BF16).reshape(owners * PIECE, head)
        landing = piece(ret, pair, me)

        def send(i, carry):
            other = lax.rem(me + i, owners)
            remote(
                piece(tot, pair, other), landing, r_send.at[pair], r_recv.at[pair], other, seq
            ).start()
            return carry

        lax.fori_loop(1, owners, send, 0)
        pltpu.make_async_copy(piece(tot, pair, me), landing, r_recv.at[pair]).start()

    def turn(g):
        limit = length_ref[0] - seq * events

        def some(i, carry):
            at = pl.ds(pl.multiple_of(i * block, block), block)
            event = i * block + lax.broadcasted_iota(jnp.int32, (block, head), 0)
            for f in range(FOLD):
                cols = slice((f * GROUPS + g) * head, (f * GROUPS + g + 1) * head)
                values = jnp.where(event < limit, raw[at, cols].astype(F32), 0.0)
                vt[cols, at] = jnp.transpose(values).astype(BF16)
            return carry

        lax.fori_loop(0, blocks, some, 0)

    def cols(g, f):
        return pl.ds(pl.multiple_of((f * GROUPS + g) * head, head), head)

    def finish(f, total):
        back = jnp.transpose(total)
        for j in range(4):
            pf[j, :, f] = back[j * span:(j + 1) * span].reshape(per, CAP, head)

    def settle(g, f, e, weight):
        return dot(vt[cols(g, f), e * block:(e + 1) * block], weight)

    def settle_late(g, c):
        finish(FOLD - 1, sums[...] + settle(g, FOLD - 1, blocks - 1, late[...]))
        part[g, c] = pf[...].reshape(4, per * PIECE, head).astype(BF16)

    def attend(g, c, last_g, last_c):
        before, after = lax.rem(seq - c + RING, RING), lax.rem(seq + c, RING)

        def columns(f):
            parts = [
                xc[g, which, s].astype(F32).reshape(-1, FOLD, CAP, head)[:, f].reshape(-1, head)
                for which, s in ((low, before), (high, after))
            ]
            return jnp.concatenate(parts, axis=0).astype(BF16)

        def weigh(f, e, queries):
            score = lax.dot_general(
                keys[e * block:(e + 1) * block, cols(g, f)], queries, (((1,), (1,)), ((), ())),
                preferred_element_type=F32,
            )
            return (score + score * jnp.tanh(score)).astype(BF16)

        queries = [columns(f) for f in range(FOLD)]
        waiting = None
        total = None
        for f in range(FOLD):
            for e in range(blocks):
                weight = weigh(f, e, queries[f])
                if waiting is None:
                    settle_late(last_g, last_c)
                else:
                    term = settle(g, *waiting)
                    total = term if waiting[1] == 0 else total + term
                    if waiting[1] == blocks - 1:
                        finish(waiting[0], total)
                waiting = (f, e, weight)
        sums[...] = total
        late[...] = waiting[2]

    def run(units, lates, after):
        def digits(values):
            numbers = [values[i:i + 8] for i in range(0, len(values), 8)]
            return [sum(v * 4 ** i for i, v in enumerate(number)) for number in numbers]

        columns = list(zip(*units)) + list(zip(*lates))
        numbers = [digits(column) for column in columns]

        def step(n, carry):
            attend(*[lax.rem(number, 4) for number in carry])

            def pick(acts, start, stop):
                if stop - start == 1:
                    for act, *args in acts[start]:
                        act(*args)
                    return
                mid = (start + stop) // 2
                for test, lo, hi in ((n < mid, start, mid), (n >= mid, mid, stop)):
                    some = {k: v for k, v in acts.items() if lo <= k < hi}
                    if some:
                        pl.when(test)(functools.partial(pick, some, lo, hi))

            pick(after, 0, len(units))
            turn_over = (n + 1) // 8 - n // 8
            return tuple(
                number // 4 + turn_over * second
                for number, (_, second) in zip(carry, numbers)
            )

        lax.fori_loop(0, len(units), step, tuple(jnp.int32(first) for first, _ in numbers))

    def gates():
        load_wg.wait()
        gated = dot(cand_ref[...], wg[...])
        gate[...] = gated / (1.0 + jnp.exp(-gated))

    scatter(0)
    for load in load_wq[FOLD:]:
        load.wait()
    others = [project(f, 1, GROUPS) for f in range(FOLD)]
    for f in range(FOLD):
        rawq[seq, :, f * head:(f + 1) * head] = others[f][:, (RAW - 1) * head:RAW * head]
    seats[seq] = jnp.broadcast_to(place_lane.astype(F32), (8, rows))
    raw_near()
    packed = pack(place_lane, others)
    for g in range(1, GROUPS):
        if g != RAW:
            fold[g] = packed[:, (g - 1) * head:g * head]
            scatter(g)
    late[...] = jnp.zeros_like(late)
    sums[...] = jnp.zeros_like(sums)
    load_v.wait()
    for g in range(GROUPS):
        turn(g)
    gates()
    await_own(0)
    pass_near(0)
    pass_rest(0)
    load_k.wait()
    units = [
        (0, OWN), (1, OWN), (0, NEAR), (0, REST), (1, NEAR), (0, FAR), (1, REST), (1, FAR),
        (3, FAR), (3, REST), (2, FAR), (2, REST), (3, NEAR), (2, NEAR), (3, OWN), (2, OWN),
    ]
    lates = [units[0]] + units[:-1]
    lates[14] = units[15]
    run(units, lates, {
        0: [(await_own, 1), (pass_near, 1), (raw_far,)],
        1: [
            (await_near, 0), (pass_far, 0), (pass_rest, 1), (await_own, 3),
            (pass_near, 3),
        ],
        2: [(await_rest, 0)],
        3: [(give_near, 0), (await_near, 1), (pass_far, 1), (scatter_raw,)],
        4: [(await_far, 0), (await_near, 3), (pass_far, 3), (pass_rest, 3)],
        5: [(await_rest, 1), (give_near, 1)],
        6: [(give_far, 0), (await_far, 1)],
        7: [(await_far, 3)],
        8: [(give_far, 1), (await_rest, 3)],
        9: [(give_far, 3), (give_rest, 0), (await_raw,)],
        11: [(give_far, 2), (give_rest, 1)],
        12: [(give_rest, 3)],
        13: [(settle_late, *units[13]), (give_near, 3), (give_near, 2)],
        14: [(give_rest, 2), (hand_back, 0)],
    })
    settle_late(*units[15])
    hand_back(1)

    place_row = jnp.transpose(
        jnp.broadcast_to(place_lane.astype(F32), (rows, rows))
    ).astype(jnp.int32)[:, :1]
    slot_lane = lax.broadcasted_iota(jnp.int32, (rows, owners * PIECE), 1)
    picks = [
        jnp.where(slot_lane == place_row + CAP * f, 1.0, 0.0).astype(BF16) for f in range(FOLD)
    ]
    load_wo.wait()

    for pair in range(GROUPS // 2):
        await_bytes(ret.at[pair], r_recv.at[pair])
    attended = jnp.concatenate(
        [dot(pick, ret[pair]) for pick in picks for pair in range(GROUPS // 2)], axis=1
    )
    centred = attended - jnp.mean(attended, axis=1, keepdims=True)
    normed = centred * lax.rsqrt(jnp.mean(centred * centred, axis=1, keepdims=True) + 1e-05)
    mixed = (normed * gate[...]).astype(BF16)
    out_ref[...] = dot(mixed, wo[...])

    sent = pl.ds(0, (owners - 1) * PIECE)
    for pair in range(GROUPS // 2):
        await_bytes(tot.at[pair, sent], r_send.at[pair])
    await_bytes(wide.at[pl.ds(0, owners - 1)], in_send.at[RAW])
    for kind in range(2):
        await_bytes(rawq.at[0], w_send.at[kind])
    for kind in range(4, 6):
        await_bytes(rawq.at[0, lower], w_send.at[kind])
    for kind in (2, 3, 6):
        await_bytes(seats.at[0], w_send.at[kind])
    for g in range(GROUPS):
        for kind in range(6):
            await_bytes(part.at[g, OWN, first], p_send.at[g * 6 + kind])
            if g != RAW:
                await_bytes(xc.at[g, low, 0], x_send.at[g * 6 + kind])
        if g != RAW:
            await_bytes(fold.at[g, sent], in_send.at[g])


def body(cand, route, lengths, keys, values, wq, wg, wo):
    owners = lax.axis_size("owner")
    rows, width = cand.shape
    head = width // HEADS
    events = keys.shape[1]
    per = owners // 4
    square = pltpu.VMEM((width, width), BF16)
    slots = pltpu.VMEM((GROUPS, owners * PIECE, head), BF16)
    pairs = pltpu.VMEM((GROUPS // 2, owners * PIECE, 2 * head), BF16)
    blocks = lambda *lead: pltpu.VMEM((GROUPS, *lead, per * PIECE, head), BF16)
    sems = lambda n: pltpu.SemaphoreType.DMA((n,))
    vmem = pl.BlockSpec(memory_space=pltpu.VMEM)
    hbm = pl.BlockSpec(memory_space=pl.ANY)
    change = pl.pallas_call(
        functools.partial(layer_kernel, owners),
        out_shape=jax.ShapeDtypeStruct((rows, width), F32),
        in_specs=[pl.BlockSpec(memory_space=pltpu.SMEM), vmem, vmem, hbm, hbm, hbm, hbm, hbm],
        out_specs=vmem,
        scratch_shapes=[
            pltpu.VMEM((events, width), BF16),
            pltpu.VMEM((events, width), BF16),
            pltpu.VMEM((width, events), BF16),
            square, square, square,
            slots,
            pltpu.VMEM((owners, RING, PIECE, head), BF16),
            pltpu.VMEM((RING, rows, FOLD * head), BF16),
            pltpu.VMEM((RING, 8, rows), F32),
            pltpu.VMEM((GROUPS, owners, RING, PIECE, head), BF16),
            blocks(4, 4),
            pltpu.VMEM((4, per, FOLD, CAP, head), F32),
            pltpu.VMEM((min(EVENT_BLOCK, events), 4 * per * CAP), BF16),
            pltpu.VMEM((head, 4 * per * CAP), F32),
            blocks(4), blocks(4), blocks(2), blocks(2),
            pairs,
            pairs,
            pltpu.VMEM((rows, width), F32),
            sems(8), sems(GROUPS), sems(GROUPS), sems(7), sems(7), sems(6 * GROUPS), sems(6 * GROUPS),
            sems(6 * GROUPS), sems(6 * GROUPS), sems(2), sems(2),
        ],
        compiler_params=pltpu.CompilerParams(
            collective_id=0, has_side_effects=True, vmem_limit_bytes=56 * 2**20
        ),
        name="candidate_layer",
    )(lengths, cand, route.reshape(1, rows), wq, wg, wo, keys, values)
    return (cand.astype(F32) + change).astype(BF16)


def solution(mesh):
    placed = (
        P(("owner", "seq"), None),
        P(("owner", "seq")),
        P("owner"),
        P("owner", "seq", None),
        P("owner", "seq", None),
        P(),
        P(),
        P(),
    )
    return jax.shard_map(
        body, mesh=mesh, in_specs=placed, out_specs=P(("owner", "seq"), None), check_vma=False
    )
```

```python
import functools

import jax
import jax.numpy as jnp
from jax import lax
from jax.experimental import pallas as pl
from jax.experimental.pallas import tpu as pltpu
from jax.sharding import PartitionSpec as P

HEADS = 8
CAP = 8
FOLD = 2
PIECE = CAP * FOLD
RING = 4
GROUPS = HEADS // FOLD
RAW = 2
OWN, NEAR, FAR, REST = range(RING)
EVENT_BLOCK = 1024
MESH = pl.DeviceIdType.MESH
F32 = jnp.float32
BF16 = jnp.bfloat16


def dot(a, b):
    return jnp.dot(a, b, preferred_element_type=F32)


def layer_kernel(
    owners,
    length_ref, cand_ref, route_ref, wq_hbm, wg_hbm, wo_hbm, k_hbm, v_hbm,
    out_ref,
    keys, raw, vt, wq, wg, wo, fold, wide, rawq, seats, xc, part, pf, late, sums, gl, gr, rl, rr, tot, ret,
    gate,
    load_sem, in_send, in_recv, w_send, w_recv, x_send, x_recv, p_send, p_recv, r_send, r_recv,
):
    me = lax.axis_index("owner")
    seq = lax.axis_index("seq")
    right, left = lax.rem(seq + 1, RING), lax.rem(seq + RING - 1, RING)
    per = owners // 4
    rows, width = cand_ref.shape
    head = width // HEADS
    events = keys.shape[0]
    block = min(EVENT_BLOCK, events)
    blocks = events // block
    span = per * CAP

    half = width // FOLD
    lead = [(slice(None), slice(f * half, f * half + head)) for f in range(FOLD)]
    rest = [(slice(None), slice(f * half + head, (f + 1) * half)) for f in range(FOLD)]
    loads = [
        pltpu.make_async_copy(src, dst, load_sem.at[i])
        for i, (src, dst) in enumerate(
            [(wq_hbm.at[part_of], wq.at[part_of]) for part_of in lead + rest]
            + [(v_hbm.at[0], raw), (wg_hbm, wg), (k_hbm.at[0], keys), (wo_hbm, wo)]
        )
    ]
    load_wq, (load_v, load_wg, load_k, load_wo) = loads[:2 * FOLD], loads[2 * FOLD:]
    for load in loads:
        load.start()

    barrier = pltpu.get_barrier_semaphore()

    def greet(i, carry):
        other = lax.rem(me + i, owners)
        pl.semaphore_signal(barrier, inc=1, device_id=(other, seq), device_id_type=MESH)
        return carry

    lax.fori_loop(1, owners, greet, 0)
    for other in (left, right):
        pl.semaphore_signal(barrier, inc=1, device_id=(me, other), device_id_type=MESH)

    def remote(src, dst, send, recv, owner, place):
        return pltpu.make_async_remote_copy(
            src_ref=src, dst_ref=dst, send_sem=send, recv_sem=recv,
            device_id=(owner, place), device_id_type=MESH,
        )

    def await_bytes(ref, sem):
        pltpu.make_async_copy(ref, ref, sem).wait()

    route_lane = jnp.broadcast_to(route_ref[...].astype(F32), (rows, rows))
    route_row = jnp.transpose(route_lane)
    lane = lax.broadcasted_iota(jnp.int32, (rows, rows), 1)
    sub = lax.broadcasted_iota(jnp.int32, (rows, rows), 0)
    same = route_lane == route_row
    before = jnp.sum(jnp.where(same & (sub < lane), 1.0, 0.0), axis=0, keepdims=True)
    place_lane = (route_ref[...].astype(F32) * PIECE + before).astype(jnp.int32)
    slot = lax.broadcasted_iota(jnp.int32, (owners * PIECE, rows), 0)

    scale = 0.5 * head ** (-0.5)

    def project(f, low, high):
        at = slice(f * half + low * head, f * half + high * head)
        return (dot(cand_ref[...], wq[:, at]) * scale).astype(BF16)

    def pack(places, queries):
        return sum(
            dot(jnp.where(slot == places + CAP * f, 1.0, 0.0).astype(BF16), queries[f])
            for f in range(FOLD)
        ).astype(BF16)

    for load in load_wq[:FOLD]:
        load.wait()
    fold[0] = pack(place_lane, [project(f, 0, 1) for f in range(FOLD)])

    pl.semaphore_wait(barrier, owners + 1)

    def piece(ref, g, owner):
        return ref.at[g, pl.ds(pl.multiple_of(owner * PIECE, PIECE), PIECE), :]

    def scatter(g):
        home = xc.at[g, me, seq]

        def send(i, carry):
            other = lax.rem(me + i, owners)
            remote(piece(fold, g, other), home, in_send.at[g], in_recv.at[g], other, seq).start()
            return carry

        lax.fori_loop(1, owners, send, 0)
        pltpu.make_async_copy(piece(fold, g, me), home, in_recv.at[g]).start()

    def await_own(g):
        await_bytes(xc.at[g, :, 0], in_recv.at[g])

    def pass_raw(kind, ref, place):
        remote(ref, ref, w_send.at[kind], w_recv.at[kind], me, place).start()

    def raw_near():
        pass_raw(0, rawq.at[seq], right)
        pass_raw(1, rawq.at[seq], left)
        pass_raw(2, seats.at[seq], right)
        pass_raw(3, seats.at[seq], left)

    lower, upper = pl.ds(0, rows // 2), pl.ds(rows // 2, rows // 2)

    def raw_far():
        for kind in range(2):
            await_bytes(rawq.at[0], w_recv.at[kind])
        for kind in range(2, 4):
            await_bytes(seats.at[0], w_recv.at[kind])
        pass_raw(4, rawq.at[left, lower], right)
        pass_raw(5, rawq.at[right, upper], left)
        pass_raw(6, seats.at[left], right)

    def scatter_raw():
        for kind in range(4, 6):
            await_bytes(rawq.at[0, lower], w_recv.at[kind])
        await_bytes(seats.at[0], w_recv.at[6])
        for s in range(RING):
            queries = [rawq[s, :, f * head:(f + 1) * head] for f in range(FOLD)]
            packed = pack(seats[s, 0:1, :].astype(jnp.int32), queries)
            wide[:, s] = packed.reshape(owners, PIECE, head)

        def send(i, carry):
            other = lax.rem(me + i, owners)
            remote(
                wide.at[other], xc.at[RAW, me], in_send.at[RAW], in_recv.at[RAW], other, seq
            ).start()
            return carry

        lax.fori_loop(1, owners, send, 0)
        pltpu.make_async_copy(wide.at[me], xc.at[RAW, me], in_recv.at[RAW]).start()

    def await_raw():
        await_bytes(xc.at[RAW], in_recv.at[RAW])

    first, last = pl.ds(0, 2), pl.ds(2, 2)
    low, high = pl.ds(0, owners // 2), pl.ds(owners // 2, owners // 2)

    def pass_on(g, kind, which, source, place):
        ref = xc.at[g, which, source]
        remote(
            ref, ref, x_send.at[g * 6 + kind], x_recv.at[g * 6 + kind], me, place
        ).start()

    def pass_near(g):
        pass_on(g, 0, low, seq, right)
        pass_on(g, 1, high, seq, left)

    def pass_rest(g):
        pass_on(g, 4, high, seq, right)
        pass_on(g, 5, low, seq, left)

    def pass_far(g):
        pass_on(g, 2, low, left, right)
        pass_on(g, 3, high, right, left)

    def await_pair(g, kind):
        await_bytes(xc.at[g, low, 0], x_recv.at[g * 6 + kind])

    def await_near(g):
        await_pair(g, 0)
        await_pair(g, 1)

    def await_far(g):
        await_pair(g, 2)
        await_pair(g, 3)

    def await_rest(g):
        await_pair(g, 4)
        await_pair(g, 5)

    def give(g, kind, source, pair, dest, place):
        remote(
            part.at[g, source, pair], dest, p_send.at[g * 6 + kind], p_recv.at[g * 6 + kind],
            me, place,
        ).start()

    def give_near(g):
        give(g, 0, NEAR, last, gl.at[g, last], right)
        give(g, 1, NEAR, first, gr.at[g, first], left)

    def give_far(g):
        give(g, 2, FAR, first, rl.at[g], right)
        give(g, 3, FAR, last, rr.at[g], left)

    def await_part(g, kind):
        await_bytes(rl.at[g], p_recv.at[g * 6 + kind])

    def give_rest(g):
        await_part(g, 2)
        part[g, REST, 0:2] = (part[g, REST, 0:2].astype(F32) + rl[g].astype(F32)).astype(BF16)
        give(g, 4, REST, first, gl.at[g, first], right)
        await_part(g, 3)
        part[g, REST, 2:4] = (part[g, REST, 2:4].astype(F32) + rr[g].astype(F32)).astype(BF16)
        give(g, 5, REST, last, gr.at[g, last], left)

    def hand_back(pair):
        for g in (2 * pair, 2 * pair + 1):
            for kind in (0, 1, 4, 5):
                await_part(g, kind)
            total = part[g, OWN].astype(F32) + gl[g].astype(F32) + gr[g].astype(F32)
            at = slice(g % 2 * head, (g % 2 + 1) * head)
            tot[pair, :, at] = total.astype(BF16).reshape(owners * PIECE, head)
        landing = piece(ret, pair, me)

        def send(i, carry):
            other = lax.rem(me + i, owners)
            remote(
                piece(tot, pair, other), landing, r_send.at[pair], r_recv.at[pair], other, seq
            ).start()
            return carry

        lax.fori_loop(1, owners, send, 0)
        pltpu.make_async_copy(piece(tot, pair, me), landing, r_recv.at[pair]).start()

    def turn(g):
        limit = length_ref[0] - seq * events

        def some(i, carry):
            at = pl.ds(pl.multiple_of(i * block, block), block)
            event = i * block + lax.broadcasted_iota(jnp.int32, (1, block), 1)
            kept = jnp.where(event < limit, 1.0, 0.0).astype(BF16)
            for f in range(FOLD):
                cols = slice((f * GROUPS + g) * head, (f * GROUPS + g + 1) * head)
                vt[cols, at] = jnp.transpose(raw[at, cols]) * kept
            return carry

        lax.fori_loop(0, blocks, some, 0)

    def cols(g, f):
        return pl.ds(pl.multiple_of((f * GROUPS + g) * head, head), head)

    def finish(f, total):
        back = jnp.transpose(total)
        for j in range(4):
            pf[j, :, f] = back[j * span:(j + 1) * span].reshape(per, CAP, head)

    def settle(g, f, e, weight):
        return dot(vt[cols(g, f), e * block:(e + 1) * block], weight)

    def settle_late(g, c):
        finish(FOLD - 1, sums[...] + settle(g, FOLD - 1, blocks - 1, late[...]))
        part[g, c] = pf[...].reshape(4, per * PIECE, head).astype(BF16)

    def attend(g, c, last_g, last_c):
        before, after = lax.rem(seq - c + RING, RING), lax.rem(seq + c, RING)

        def columns(f):
            parts = [
                xc[g, which, s].astype(F32).reshape(-1, FOLD, CAP, head)[:, f].reshape(-1, head)
                for which, s in ((low, before), (high, after))
            ]
            return jnp.concatenate(parts, axis=0).astype(BF16)

        def weigh(f, e, queries):
            score = lax.dot_general(
                keys[e * block:(e + 1) * block, cols(g, f)], queries, (((1,), (1,)), ((), ())),
                preferred_element_type=F32,
            )
            return (score + score * jnp.tanh(score)).astype(BF16)

        queries = [columns(f) for f in range(FOLD)]
        waiting = None
        total = None
        for f in range(FOLD):
            for e in range(blocks):
                weight = weigh(f, e, queries[f])
                if waiting is None:
                    settle_late(last_g, last_c)
                else:
                    term = settle(g, *waiting)
                    total = term if waiting[1] == 0 else total + term
                    if waiting[1] == blocks - 1:
                        finish(waiting[0], total)
                waiting = (f, e, weight)
        sums[...] = total
        late[...] = waiting[2]

    def run(units, lates, after):
        def digits(values):
            numbers = [values[i:i + 8] for i in range(0, len(values), 8)]
            return [sum(v * 4 ** i for i, v in enumerate(number)) for number in numbers]

        columns = list(zip(*units)) + list(zip(*lates))
        numbers = [digits(column) for column in columns]

        def step(n, carry):
            attend(*[lax.rem(number, 4) for number in carry])

            def pick(acts, start, stop):
                if stop - start == 1:
                    for act, *args in acts[start]:
                        act(*args)
                    return
                mid = (start + stop) // 2
                for test, lo, hi in ((n < mid, start, mid), (n >= mid, mid, stop)):
                    some = {k: v for k, v in acts.items() if lo <= k < hi}
                    if some:
                        pl.when(test)(functools.partial(pick, some, lo, hi))

            pick(after, 0, len(units))
            turn_over = (n + 1) // 8 - n // 8
            return tuple(
                number // 4 + turn_over * second
                for number, (_, second) in zip(carry, numbers)
            )

        lax.fori_loop(0, len(units), step, tuple(jnp.int32(first) for first, _ in numbers))

    def gates():
        load_wg.wait()
        gated = dot(cand_ref[...], wg[...])
        gate[...] = gated / (1.0 + jnp.exp(-gated))

    scatter(0)
    for load in load_wq[FOLD:]:
        load.wait()
    others = [project(f, 1, GROUPS) for f in range(FOLD)]
    for f in range(FOLD):
        rawq[seq, :, f * head:(f + 1) * head] = others[f][:, (RAW - 1) * head:RAW * head]
    seats[seq] = jnp.broadcast_to(place_lane.astype(F32), (8, rows))
    raw_near()
    packed = pack(place_lane, others)
    for g in range(1, GROUPS):
        if g != RAW:
            fold[g] = packed[:, (g - 1) * head:g * head]
            scatter(g)
    late[...] = jnp.zeros_like(late)
    sums[...] = jnp.zeros_like(sums)
    load_v.wait()
    for g in range(GROUPS):
        turn(g)
    await_own(0)
    pass_near(0)
    pass_rest(0)
    load_k.wait()
    units = [
        (0, OWN), (1, OWN), (0, NEAR), (0, REST), (1, NEAR), (0, FAR), (1, REST), (1, FAR),
        (3, FAR), (3, REST), (2, FAR), (2, REST), (3, NEAR), (2, NEAR), (3, OWN), (2, OWN),
    ]
    lates = [units[0]] + units[:-1]
    lates[14] = units[15]
    run(units, lates, {
        0: [(await_own, 1), (pass_near, 1), (raw_far,)],
        1: [
            (await_near, 0), (pass_far, 0), (pass_rest, 1), (await_own, 3),
            (pass_near, 3),
        ],
        2: [(await_rest, 0)],
        3: [(give_near, 0), (await_near, 1), (pass_far, 1), (scatter_raw,)],
        4: [(await_far, 0), (await_near, 3), (pass_far, 3), (pass_rest, 3)],
        5: [(await_rest, 1), (give_near, 1)],
        6: [(give_far, 0), (await_far, 1)],
        7: [(await_far, 3)],
        8: [(give_far, 1), (await_rest, 3)],
        9: [(give_far, 3), (give_rest, 0), (await_raw,)],
        11: [(give_far, 2), (give_rest, 1)],
        12: [(give_rest, 3)],
        13: [(settle_late, *units[13]), (give_near, 3), (give_near, 2)],
        14: [(give_rest, 2), (hand_back, 0)],
    })
    settle_late(*units[15])
    hand_back(1)

    sent = pl.ds(0, (owners - 1) * PIECE)
    await_bytes(wide.at[pl.ds(0, owners - 1)], in_send.at[RAW])
    for kind in range(2):
        await_bytes(rawq.at[0], w_send.at[kind])
    for kind in range(4, 6):
        await_bytes(rawq.at[0, lower], w_send.at[kind])
    for kind in (2, 3, 6):
        await_bytes(seats.at[0], w_send.at[kind])
    for g in range(GROUPS):
        for kind in range(6):
            await_bytes(part.at[g, OWN, first], p_send.at[g * 6 + kind])
            if g != RAW:
                await_bytes(xc.at[g, low, 0], x_send.at[g * 6 + kind])
        if g != RAW:
            await_bytes(fold.at[g, sent], in_send.at[g])
    gates()
    place_row = jnp.transpose(
        jnp.broadcast_to(place_lane.astype(F32), (rows, rows))
    ).astype(jnp.int32)[:, :1]
    slot_lane = lax.broadcasted_iota(jnp.int32, (rows, owners * PIECE), 1)
    picks = [
        jnp.where(slot_lane == place_row + CAP * f, 1.0, 0.0).astype(BF16) for f in range(FOLD)
    ]
    load_wo.wait()

    returned = []
    for pair in range(GROUPS // 2):
        await_bytes(ret.at[pair], r_recv.at[pair])
        returned.append([dot(pick, ret[pair]) for pick in picks])
    attended = jnp.concatenate([rows_of[f] for f in range(FOLD) for rows_of in returned], axis=1)
    centred = attended - jnp.mean(attended, axis=1, keepdims=True)
    normed = centred * lax.rsqrt(jnp.mean(centred * centred, axis=1, keepdims=True) + 1e-05)
    mixed = (normed * gate[...]).astype(BF16)
    out_ref[...] = (cand_ref[...].astype(F32) + dot(mixed, wo[...])).astype(BF16)
    for pair in range(GROUPS // 2):
        await_bytes(tot.at[pair, sent], r_send.at[pair])


def body(cand, route, lengths, keys, values, wq, wg, wo):
    owners = lax.axis_size("owner")
    rows, width = cand.shape
    head = width // HEADS
    events = keys.shape[1]
    per = owners // 4
    square = pltpu.VMEM((width, width), BF16)
    slots = pltpu.VMEM((GROUPS, owners * PIECE, head), BF16)
    pairs = pltpu.VMEM((GROUPS // 2, owners * PIECE, 2 * head), BF16)
    blocks = lambda *lead: pltpu.VMEM((GROUPS, *lead, per * PIECE, head), BF16)
    sems = lambda n: pltpu.SemaphoreType.DMA((n,))
    vmem = pl.BlockSpec(memory_space=pltpu.VMEM)
    hbm = pl.BlockSpec(memory_space=pl.ANY)
    return pl.pallas_call(
        functools.partial(layer_kernel, owners),
        out_shape=jax.ShapeDtypeStruct((rows, width), BF16),
        in_specs=[pl.BlockSpec(memory_space=pltpu.SMEM), vmem, vmem, hbm, hbm, hbm, hbm, hbm],
        out_specs=vmem,
        scratch_shapes=[
            pltpu.VMEM((events, width), BF16),
            pltpu.VMEM((events, width), BF16),
            pltpu.VMEM((width, events), BF16),
            square, square, square,
            slots,
            pltpu.VMEM((owners, RING, PIECE, head), BF16),
            pltpu.VMEM((RING, rows, FOLD * head), BF16),
            pltpu.VMEM((RING, 8, rows), F32),
            pltpu.VMEM((GROUPS, owners, RING, PIECE, head), BF16),
            blocks(4, 4),
            pltpu.VMEM((4, per, FOLD, CAP, head), F32),
            pltpu.VMEM((min(EVENT_BLOCK, events), 4 * per * CAP), BF16),
            pltpu.VMEM((head, 4 * per * CAP), F32),
            blocks(4), blocks(4), blocks(2), blocks(2),
            pairs,
            pairs,
            pltpu.VMEM((rows, width), F32),
            sems(8), sems(GROUPS), sems(GROUPS), sems(7), sems(7), sems(6 * GROUPS), sems(6 * GROUPS),
            sems(6 * GROUPS), sems(6 * GROUPS), sems(2), sems(2),
        ],
        compiler_params=pltpu.CompilerParams(
            collective_id=0, has_side_effects=True, vmem_limit_bytes=56 * 2**20
        ),
        name="candidate_layer",
    )(lengths, cand, route.reshape(1, rows), wq, wg, wo, keys, values)


def solution(mesh):
    placed = (
        P(("owner", "seq"), None),
        P(("owner", "seq")),
        P("owner"),
        P("owner", "seq", None),
        P("owner", "seq", None),
        P(),
        P(),
        P(),
    )
    return jax.shard_map(
        body, mesh=mesh, in_specs=placed, out_specs=P(("owner", "seq"), None), check_vma=False
    )
```

```python
import functools

import jax
import jax.numpy as jnp
from jax import lax
from jax.experimental import pallas as pl
from jax.experimental.pallas import tpu as pltpu
from jax.sharding import PartitionSpec as P

HEADS = 8
CAP = 8
FOLD = 2
PIECE = CAP * FOLD
RING = 4
GROUPS = HEADS // FOLD
RAW = 2
OWN, NEAR, FAR, REST = range(RING)
EVENT_BLOCK = 1024
MESH = pl.DeviceIdType.MESH
F32 = jnp.float32
BF16 = jnp.bfloat16


def dot(a, b):
    return jnp.dot(a, b, preferred_element_type=F32)


def layer_kernel(
    owners,
    length_ref, cand_ref, route_ref, wq_hbm, wg_hbm, wo_hbm, k_hbm, v_hbm,
    out_ref,
    keys, raw, vt, wq, wg, wo, fold, wide, rawq, seats, xc, part, pf, late, sums, gl, gr, rl, rr, tot, ret,
    gate,
    load_sem, in_send, in_recv, w_send, w_recv, x_send, x_recv, p_send, p_recv, r_send, r_recv,
):
    me = lax.axis_index("owner")
    seq = lax.axis_index("seq")
    right, left = lax.rem(seq + 1, RING), lax.rem(seq + RING - 1, RING)
    per = owners // 4
    rows, width = cand_ref.shape
    head = width // HEADS
    events = keys.shape[0]
    block = min(EVENT_BLOCK, events)
    blocks = events // block
    span = per * CAP

    half = width // FOLD
    lead = [(slice(None), slice(f * half, f * half + head)) for f in range(FOLD)]
    rest = [(slice(None), slice(f * half + head, (f + 1) * half)) for f in range(FOLD)]
    loads = [
        pltpu.make_async_copy(src, dst, load_sem.at[i])
        for i, (src, dst) in enumerate(
            [(wq_hbm.at[part_of], wq.at[part_of]) for part_of in lead + rest]
            + [(v_hbm.at[0], raw), (wg_hbm, wg), (k_hbm.at[0], keys), (wo_hbm, wo)]
        )
    ]
    load_wq, (load_v, load_wg, load_k, load_wo) = loads[:2 * FOLD], loads[2 * FOLD:]
    for load in loads:
        load.start()

    barrier = pltpu.get_barrier_semaphore()

    def greet(i, carry):
        other = lax.rem(me + i, owners)
        pl.semaphore_signal(barrier, inc=1, device_id=(other, seq), device_id_type=MESH)
        return carry

    lax.fori_loop(1, owners, greet, 0)
    for other in (left, right):
        pl.semaphore_signal(barrier, inc=1, device_id=(me, other), device_id_type=MESH)

    def remote(src, dst, send, recv, owner, place):
        return pltpu.make_async_remote_copy(
            src_ref=src, dst_ref=dst, send_sem=send, recv_sem=recv,
            device_id=(owner, place), device_id_type=MESH,
        )

    def await_bytes(ref, sem):
        pltpu.make_async_copy(ref, ref, sem).wait()

    route_lane = jnp.broadcast_to(route_ref[...].astype(F32), (rows, rows))
    route_row = jnp.transpose(route_lane)
    lane = lax.broadcasted_iota(jnp.int32, (rows, rows), 1)
    sub = lax.broadcasted_iota(jnp.int32, (rows, rows), 0)
    same = route_lane == route_row
    before = jnp.sum(jnp.where(same & (sub < lane), 1.0, 0.0), axis=0, keepdims=True)
    place_lane = (route_ref[...].astype(F32) * PIECE + before).astype(jnp.int32)
    slot = lax.broadcasted_iota(jnp.int32, (owners * PIECE, rows), 0)

    scale = 0.5 * head ** (-0.5)

    def project(f, low, high):
        at = slice(f * half + low * head, f * half + high * head)
        return (dot(cand_ref[...], wq[:, at]) * scale).astype(BF16)

    def pack(places, queries):
        return sum(
            dot(jnp.where(slot == places + CAP * f, 1.0, 0.0).astype(BF16), queries[f])
            for f in range(FOLD)
        ).astype(BF16)

    for load in load_wq[:FOLD]:
        load.wait()
    fold[0] = pack(place_lane, [project(f, 0, 1) for f in range(FOLD)])

    pl.semaphore_wait(barrier, owners + 1)

    def piece(ref, g, owner):
        return ref.at[g, pl.ds(pl.multiple_of(owner * PIECE, PIECE), PIECE), :]

    def scatter(g):
        home = xc.at[g, me, seq]

        def send(i, carry):
            other = lax.rem(me + i, owners)
            remote(piece(fold, g, other), home, in_send.at[g], in_recv.at[g], other, seq).start()
            return carry

        lax.fori_loop(1, owners, send, 0)
        pltpu.make_async_copy(piece(fold, g, me), home, in_recv.at[g]).start()

    def await_own(g):
        await_bytes(xc.at[g, :, 0], in_recv.at[g])

    def pass_raw(kind, ref, place):
        remote(ref, ref, w_send.at[kind], w_recv.at[kind], me, place).start()

    def raw_near():
        pass_raw(0, rawq.at[seq], right)
        pass_raw(1, rawq.at[seq], left)
        pass_raw(2, seats.at[seq], right)
        pass_raw(3, seats.at[seq], left)

    lower, upper = pl.ds(0, rows // 2), pl.ds(rows // 2, rows // 2)

    def raw_far():
        for kind in range(2):
            await_bytes(rawq.at[0], w_recv.at[kind])
        for kind in range(2, 4):
            await_bytes(seats.at[0], w_recv.at[kind])
        pass_raw(4, rawq.at[left, lower], right)
        pass_raw(5, rawq.at[right, upper], left)
        pass_raw(6, seats.at[left], right)

    def scatter_raw():
        for kind in range(4, 6):
            await_bytes(rawq.at[0, lower], w_recv.at[kind])
        await_bytes(seats.at[0], w_recv.at[6])
        for s in range(RING):
            queries = [rawq[s, :, f * head:(f + 1) * head] for f in range(FOLD)]
            packed = pack(seats[s, 0:1, :].astype(jnp.int32), queries)
            wide[:, s] = packed.reshape(owners, PIECE, head)

        def send(i, carry):
            other = lax.rem(me + i, owners)
            remote(
                wide.at[other], xc.at[RAW, me], in_send.at[RAW], in_recv.at[RAW], other, seq
            ).start()
            return carry

        lax.fori_loop(1, owners, send, 0)
        pltpu.make_async_copy(wide.at[me], xc.at[RAW, me], in_recv.at[RAW]).start()

    def await_raw():
        await_bytes(xc.at[RAW], in_recv.at[RAW])

    first, last = pl.ds(0, 2), pl.ds(2, 2)
    low, high = pl.ds(0, owners // 2), pl.ds(owners // 2, owners // 2)

    def pass_on(g, kind, which, source, place):
        ref = xc.at[g, which, source]
        remote(
            ref, ref, x_send.at[g * 6 + kind], x_recv.at[g * 6 + kind], me, place
        ).start()

    def pass_near(g):
        pass_on(g, 0, low, seq, right)
        pass_on(g, 1, high, seq, left)

    def pass_rest(g):
        pass_on(g, 4, high, seq, right)
        pass_on(g, 5, low, seq, left)

    def pass_far(g):
        pass_on(g, 2, low, left, right)
        pass_on(g, 3, high, right, left)

    def await_pair(g, kind):
        await_bytes(xc.at[g, low, 0], x_recv.at[g * 6 + kind])

    def await_near(g):
        await_pair(g, 0)
        await_pair(g, 1)

    def await_far(g):
        await_pair(g, 2)
        await_pair(g, 3)

    def await_rest(g):
        await_pair(g, 4)
        await_pair(g, 5)

    def give(g, kind, source, pair, dest, place):
        remote(
            part.at[g, source, pair], dest, p_send.at[g * 6 + kind], p_recv.at[g * 6 + kind],
            me, place,
        ).start()

    def give_near(g):
        give(g, 0, NEAR, last, gl.at[g, last], right)
        give(g, 1, NEAR, first, gr.at[g, first], left)

    def give_far(g):
        give(g, 2, FAR, first, rl.at[g], right)
        give(g, 3, FAR, last, rr.at[g], left)

    def await_part(g, kind):
        await_bytes(rl.at[g], p_recv.at[g * 6 + kind])

    def give_rest(g):
        await_part(g, 2)
        part[g, REST, 0:2] = (part[g, REST, 0:2].astype(F32) + rl[g].astype(F32)).astype(BF16)
        give(g, 4, REST, first, gl.at[g, first], right)
        await_part(g, 3)
        part[g, REST, 2:4] = (part[g, REST, 2:4].astype(F32) + rr[g].astype(F32)).astype(BF16)
        give(g, 5, REST, last, gr.at[g, last], left)

    def hand_back(pair):
        for g in (2 * pair, 2 * pair + 1):
            for kind in (0, 1, 4, 5):
                await_part(g, kind)
            total = part[g, OWN].astype(F32) + gl[g].astype(F32) + gr[g].astype(F32)
            at = slice(g % 2 * head, (g % 2 + 1) * head)
            tot[pair, :, at] = total.astype(BF16).reshape(owners * PIECE, head)
        landing = piece(ret, pair, me)

        def send(i, carry):
            other = lax.rem(me + i, owners)
            remote(
                piece(tot, pair, other), landing, r_send.at[pair], r_recv.at[pair], other, seq
            ).start()
            return carry

        lax.fori_loop(1, owners, send, 0)
        pltpu.make_async_copy(piece(tot, pair, me), landing, r_recv.at[pair]).start()

    def turn(g):
        limit = length_ref[0] - seq * events

        def some(i, carry):
            at = pl.ds(pl.multiple_of(i * block, block), block)
            event = i * block + lax.broadcasted_iota(jnp.int32, (1, block), 1)
            kept = jnp.where(event < limit, 1.0, 0.0).astype(BF16)
            for f in range(FOLD):
                cols = slice((f * GROUPS + g) * head, (f * GROUPS + g + 1) * head)
                vt[cols, at] = jnp.transpose(raw[at, cols]) * kept
            return carry

        lax.fori_loop(0, blocks, some, 0)

    def cols(g, f):
        return pl.ds(pl.multiple_of((f * GROUPS + g) * head, head), head)

    def finish(f, total):
        back = jnp.transpose(total)
        for j in range(4):
            pf[j, :, f] = back[j * span:(j + 1) * span].reshape(per, CAP, head)

    def settle(g, f, e, weight):
        return dot(vt[cols(g, f), e * block:(e + 1) * block], weight)

    def settle_late(g, c):
        finish(FOLD - 1, sums[...] + settle(g, FOLD - 1, blocks - 1, late[...]))
        part[g, c] = pf[...].reshape(4, per * PIECE, head).astype(BF16)

    def attend(g, c, last_g, last_c):
        before, after = lax.rem(seq - c + RING, RING), lax.rem(seq + c, RING)

        def columns(f):
            parts = [
                xc[g, which, s].astype(F32).reshape(-1, FOLD, CAP, head)[:, f].reshape(-1, head)
                for which, s in ((low, before), (high, after))
            ]
            return jnp.concatenate(parts, axis=0).astype(BF16)

        def weigh(f, e, queries):
            score = lax.dot_general(
                keys[e * block:(e + 1) * block, cols(g, f)], queries, (((1,), (1,)), ((), ())),
                preferred_element_type=F32,
            )
            return (score + score * jnp.tanh(score)).astype(BF16)

        queries = [columns(f) for f in range(FOLD)]
        waiting = None
        total = None
        for f in range(FOLD):
            for e in range(blocks):
                weight = weigh(f, e, queries[f])
                if waiting is None:
                    settle_late(last_g, last_c)
                else:
                    term = settle(g, *waiting)
                    total = term if waiting[1] == 0 else total + term
                    if waiting[1] == blocks - 1:
                        finish(waiting[0], total)
                waiting = (f, e, weight)
        sums[...] = total
        late[...] = waiting[2]

    def run(units, lates, after):
        def digits(values):
            numbers = [values[i:i + 8] for i in range(0, len(values), 8)]
            return [sum(v * 4 ** i for i, v in enumerate(number)) for number in numbers]

        columns = list(zip(*units)) + list(zip(*lates))
        numbers = [digits(column) for column in columns]

        def step(n, carry):
            attend(*[lax.rem(number, 4) for number in carry])

            def pick(acts, start, stop):
                if stop - start == 1:
                    for act, *args in acts[start]:
                        act(*args)
                    return
                mid = (start + stop) // 2
                for test, lo, hi in ((n < mid, start, mid), (n >= mid, mid, stop)):
                    some = {k: v for k, v in acts.items() if lo <= k < hi}
                    if some:
                        pl.when(test)(functools.partial(pick, some, lo, hi))

            pick(after, 0, len(units))
            turn_over = (n + 1) // 8 - n // 8
            return tuple(
                number // 4 + turn_over * second
                for number, (_, second) in zip(carry, numbers)
            )

        lax.fori_loop(0, len(units), step, tuple(jnp.int32(first) for first, _ in numbers))

    def gates():
        load_wg.wait()
        gated = dot(cand_ref[...], wg[...])
        gate[...] = gated / (1.0 + jnp.exp(-gated))

    scatter(0)
    for load in load_wq[FOLD:]:
        load.wait()
    others = [project(f, 1, GROUPS) for f in range(FOLD)]
    for f in range(FOLD):
        rawq[seq, :, f * head:(f + 1) * head] = others[f][:, (RAW - 1) * head:RAW * head]
    seats[seq] = jnp.broadcast_to(place_lane.astype(F32), (8, rows))
    raw_near()
    packed = pack(place_lane, others)
    for g in range(1, GROUPS):
        if g != RAW:
            fold[g] = packed[:, (g - 1) * head:g * head]
            scatter(g)
    late[...] = jnp.zeros_like(late)
    sums[...] = jnp.zeros_like(sums)
    load_v.wait()
    for g in range(GROUPS):
        turn(g)
    await_own(0)
    pass_near(0)
    pass_rest(0)
    load_k.wait()
    units = [
        (0, OWN), (1, OWN), (0, NEAR), (0, REST), (1, NEAR), (0, FAR), (1, REST), (1, FAR),
        (3, FAR), (2, FAR), (3, NEAR), (2, NEAR), (3, REST), (2, REST), (3, OWN), (2, OWN),
    ]
    lates = [units[0]] + units[:-1]
    lates[14] = units[15]
    run(units, lates, {
        0: [(await_own, 1), (pass_near, 1), (raw_far,)],
        1: [
            (await_near, 0), (pass_far, 0), (pass_rest, 1), (await_own, 3),
            (pass_near, 3),
        ],
        2: [(await_rest, 0)],
        3: [(give_near, 0), (await_near, 1), (pass_far, 1), (scatter_raw,)],
        4: [(await_far, 0), (await_near, 3), (pass_far, 3), (pass_rest, 3)],
        5: [(await_rest, 1), (give_near, 1)],
        6: [(give_far, 0), (await_far, 1)],
        7: [(await_far, 3)],
        8: [(give_far, 1), (await_raw,)],
        9: [(give_far, 3), (give_rest, 0)],
        10: [(give_far, 2)],
        11: [(give_near, 3), (give_rest, 1), (await_rest, 3)],
        12: [(give_near, 2)],
        13: [(settle_late, *units[13]), (give_rest, 3), (give_rest, 2)],
        14: [(hand_back, 0)],
    })
    settle_late(*units[15])
    hand_back(1)

    sent = pl.ds(0, (owners - 1) * PIECE)
    await_bytes(wide.at[pl.ds(0, owners - 1)], in_send.at[RAW])
    for kind in range(2):
        await_bytes(rawq.at[0], w_send.at[kind])
    for kind in range(4, 6):
        await_bytes(rawq.at[0, lower], w_send.at[kind])
    for kind in (2, 3, 6):
        await_bytes(seats.at[0], w_send.at[kind])
    for g in range(GROUPS):
        for kind in range(6):
            await_bytes(part.at[g, OWN, first], p_send.at[g * 6 + kind])
            if g != RAW:
                await_bytes(xc.at[g, low, 0], x_send.at[g * 6 + kind])
        if g != RAW:
            await_bytes(fold.at[g, sent], in_send.at[g])
    gates()
    place_row = jnp.transpose(
        jnp.broadcast_to(place_lane.astype(F32), (rows, rows))
    ).astype(jnp.int32)[:, :1]
    slot_lane = lax.broadcasted_iota(jnp.int32, (rows, owners * PIECE), 1)
    picks = [
        jnp.where(slot_lane == place_row + CAP * f, 1.0, 0.0).astype(BF16) for f in range(FOLD)
    ]
    load_wo.wait()

    returned = []
    for pair in range(GROUPS // 2):
        await_bytes(ret.at[pair], r_recv.at[pair])
        returned.append([dot(pick, ret[pair]) for pick in picks])
    attended = jnp.concatenate([rows_of[f] for f in range(FOLD) for rows_of in returned], axis=1)
    centred = attended - jnp.mean(attended, axis=1, keepdims=True)
    normed = centred * lax.rsqrt(jnp.mean(centred * centred, axis=1, keepdims=True) + 1e-05)
    mixed = (normed * gate[...]).astype(BF16)
    out_ref[...] = (cand_ref[...].astype(F32) + dot(mixed, wo[...])).astype(BF16)
    for pair in range(GROUPS // 2):
        await_bytes(tot.at[pair, sent], r_send.at[pair])


def body(cand, route, lengths, keys, values, wq, wg, wo):
    owners = lax.axis_size("owner")
    rows, width = cand.shape
    head = width // HEADS
    events = keys.shape[1]
    per = owners // 4
    square = pltpu.VMEM((width, width), BF16)
    slots = pltpu.VMEM((GROUPS, owners * PIECE, head), BF16)
    pairs = pltpu.VMEM((GROUPS // 2, owners * PIECE, 2 * head), BF16)
    blocks = lambda *lead: pltpu.VMEM((GROUPS, *lead, per * PIECE, head), BF16)
    sems = lambda n: pltpu.SemaphoreType.DMA((n,))
    vmem = pl.BlockSpec(memory_space=pltpu.VMEM)
    hbm = pl.BlockSpec(memory_space=pl.ANY)
    return pl.pallas_call(
        functools.partial(layer_kernel, owners),
        out_shape=jax.ShapeDtypeStruct((rows, width), BF16),
        in_specs=[pl.BlockSpec(memory_space=pltpu.SMEM), vmem, vmem, hbm, hbm, hbm, hbm, hbm],
        out_specs=vmem,
        scratch_shapes=[
            pltpu.VMEM((events, width), BF16),
            pltpu.VMEM((events, width), BF16),
            pltpu.VMEM((width, events), BF16),
            square, square, square,
            slots,
            pltpu.VMEM((owners, RING, PIECE, head), BF16),
            pltpu.VMEM((RING, rows, FOLD * head), BF16),
            pltpu.VMEM((RING, 8, rows), F32),
            pltpu.VMEM((GROUPS, owners, RING, PIECE, head), BF16),
            blocks(4, 4),
            pltpu.VMEM((4, per, FOLD, CAP, head), F32),
            pltpu.VMEM((min(EVENT_BLOCK, events), 4 * per * CAP), BF16),
            pltpu.VMEM((head, 4 * per * CAP), F32),
            blocks(4), blocks(4), blocks(2), blocks(2),
            pairs,
            pairs,
            pltpu.VMEM((rows, width), F32),
            sems(8), sems(GROUPS), sems(GROUPS), sems(7), sems(7), sems(6 * GROUPS), sems(6 * GROUPS),
            sems(6 * GROUPS), sems(6 * GROUPS), sems(2), sems(2),
        ],
        compiler_params=pltpu.CompilerParams(
            collective_id=0, has_side_effects=True, vmem_limit_bytes=56 * 2**20
        ),
        name="candidate_layer",
    )(lengths, cand, route.reshape(1, rows), wq, wg, wo, keys, values)


def solution(mesh):
    placed = (
        P(("owner", "seq"), None),
        P(("owner", "seq")),
        P("owner"),
        P("owner", "seq", None),
        P("owner", "seq", None),
        P(),
        P(),
        P(),
    )
    return jax.shard_map(
        body, mesh=mesh, in_specs=placed, out_specs=P(("owner", "seq"), None), check_vma=False
    )
```
